32 devices in a mesh: lat: 16 (over z, y, core), tgt: 2 (over x).
Axes of the slice: x: 2, y: 2, z: 4, core: 2. Of those that a mesh axis runs over, the one named last changes fastest.
Arguments:
- inputs: bfloat16 [128, 2, 2304], P('lat', None, 'tgt'), may hold values from -6 to 6
- w_enc: bfloat16 [2304, 32768], P('tgt', 'lat'), may hold values from -0.125 to 0.125
- b_enc: float32 [32768], P('lat'), may hold values from -4 to 4
- masks: int32 [128, 32768], P(None, 'lat'), may hold values 0 or 1
- w_dec: bfloat16 [2, 32768, 2304], P('tgt', 'lat'), may hold values from -0.046875 to 0.046875
- errors: bfloat16 [2, 128, 2304], P('tgt', 'lat'), may hold values from -6 to 6
- target_of: int32 [2], replicated, may hold values from 0 to 1, each once
Outputs:
- grad_enc: float32 [2304, 32768], P('tgt', 'lat')
- grad_bias: float32 [32768], P('lat')
- grad_in: float32 [128, 2, 2304], P('lat', None, 'tgt')
The draws below stay inside these ranges and needn't reach their ends.
Inputs may be any that keep to these rules, and one draw needn't show every extreme that they name: `target_of`: each target layer names exactly one slot.
All inputs are finite; a program needn't handle non-finite values. No bound on the sum of `masks` on one device may be relied on, other than what follows from the above.
Results may differ from the reference program's by a relative error of at most 0.0029.
Values may be sent and summed in bfloat16 or wider, within the bound.
A program may use at most 64 MiB of HBM per device.

```python
import jax
import jax.numpy as jnp
from jax import lax

D = 2304
F = 16384
S = 2
TOKENS = 128
LATS = 32768
TGT = 2


def touch_ends(values, key, smallest, top_value):
    dims = values.shape
    spot = [jax.random.randint(jax.random.fold_in(key, axis), (), 0, dims[axis]) for axis in range(len(dims))]
    values = values.at[tuple(spot)].set(smallest)
    longest = dims.index(max(dims))
    spot[longest] = (spot[longest] + 1) % dims[longest]
    return values.at[tuple(spot)].set(top_value)


def shard_levels(key, shape, shards, low, largest):
    level = 1.0
    for axis_at, blocks in shards:
        steps = jax.random.uniform(jax.random.fold_in(jax.random.fold_in(key, 6), axis_at), (blocks,), jnp.float32, low / len(shards), largest / len(shards))
        level = level * jnp.repeat(jnp.exp(steps), shape[axis_at] // blocks).reshape((-1,) + (1,) * (len(shape) - 1 - axis_at))
    return level


def centred(stream_key, shape, width, bound, split=(), held_as=jnp.bfloat16):
    factor_of = shard_levels(stream_key, shape, split, -0.22, 0.18) if split else 1.0
    result = jax.random.normal(stream_key, shape, jnp.float32) * width * factor_of
    return jnp.minimum(jnp.maximum(result, -bound), bound).astype(held_as)


def setup_inputs(seed: int = 0) -> dict:
    arg_keys = jax.random.split(jax.random.key(seed), 8)
    inputs = centred(arg_keys[0], (TOKENS, S, D), 1.0, 6.0, ((0, 16), (2, 2)))
    w_enc = centred(arg_keys[1], (D, LATS), D ** -0.5, 0.125, ((0, 2), (1, 16)))
    b_enc = centred(arg_keys[2], (LATS,), 1.0, 4.0, ((0, 16),), jnp.float32)
    masks = touch_ends((jax.random.randint(arg_keys[3], (TOKENS, LATS), 0, 4) < 1).astype(jnp.int32), jax.random.fold_in(arg_keys[3], 1), 0, 1)
    w_dec = centred(arg_keys[4], (TGT, LATS, D), F ** -0.5, 0.046875, ((0, 2), (1, 16)))
    errors = centred(arg_keys[5], (TGT, TOKENS, D), 1.0, 6.0, ((0, 2), (1, 16)))
    target_of = jax.random.permutation(arg_keys[6], TGT).astype(jnp.int32)
    return dict(inputs=inputs, w_enc=w_enc, b_enc=b_enc, masks=masks, w_dec=w_dec, errors=errors, target_of=target_of)


penalty = 1.0
sharpness = 1.0

def reference(inputs, w_enc, b_enc, masks, w_dec, errors, target_of):
    source = jnp.arange(LATS, dtype=jnp.int32) // F
    live = (target_of[:, None] >= source[None, :]).astype(jnp.float32)
    pieces = []
    for layer in range(S):
        pieces.append(jnp.dot(inputs[:, layer, :], w_enc[:, layer * F:(layer + 1) * F], preferred_element_type=jnp.float32))
    pre = jnp.concatenate(pieces, axis=1) + b_enc[None, :]
    gates = masks.astype(jnp.float32)
    act = gates * pre
    squares = lax.map(lambda w: lax.optimization_barrier(jnp.sum(jnp.square(w.astype(jnp.float32)), axis=1)), w_dec)
    norm = jnp.sqrt(lax.optimization_barrier(jnp.sum(live * squares, axis=0)))
    dact = jnp.zeros((TOKENS, LATS), jnp.float32)
    for slot in range(TGT):
        dact = dact + live[slot][None, :] * jnp.dot(errors[slot], w_dec[slot].T, preferred_element_type=jnp.float32)
    tanh_val = jnp.tanh(sharpness * act * norm[None, :])
    grad = (gates * (dact + penalty * sharpness * norm[None, :] * (1.0 - tanh_val * tanh_val))).astype(jnp.bfloat16)
    grad_bias = lax.optimization_barrier(jnp.sum(grad.astype(jnp.float32), axis=0))
    enc_parts = []
    in_parts = []
    for layer in range(S):
        cols = grad[:, layer * F:(layer + 1) * F]
        enc_parts.append(jnp.dot(inputs[:, layer, :].T, cols, preferred_element_type=jnp.float32))
        in_parts.append(jnp.dot(cols, w_enc[:, layer * F:(layer + 1) * F].T, preferred_element_type=jnp.float32))
    grad_enc = jnp.concatenate(enc_parts, axis=1)
    grad_in = jnp.stack(in_parts, axis=1)
    return (grad_enc, grad_bias, grad_in)
```

```python
import functools

import jax
import jax.numpy as jnp
from jax import lax
from jax.experimental import pallas as pl
from jax.experimental.pallas import tpu as pltpu
from jax.sharding import PartitionSpec as P

F = 16384
S = 2
MESH = pl.DeviceIdType.MESH
Z = 4
NT = 4
TILE = 256

penalty = 1.0
sharpness = 1.0


def latent_grad(dact, sumsq, act, gates):
    norm = jnp.sqrt(sumsq)[None, :]
    tanh_val = jnp.tanh(sharpness * act * norm)
    return (gates * (dact + penalty * sharpness * norm * (1.0 - tanh_val * tanh_val))).astype(
        jnp.bfloat16
    )


def local_any(inputs, w_enc, b_enc, masks, w_dec, errors, target_of):
    block = w_enc.shape[1]
    source = lax.axis_index("lat") * block // F
    slot = lax.axis_index("tgt")
    slots = jnp.arange(target_of.shape[0], dtype=jnp.int32)
    layer = jnp.sum(jnp.where(slots == slot, target_of, 0))
    flag = (layer >= source).astype(jnp.float32)
    gathered = lax.all_gather(inputs, "lat", axis=0, tiled=True)
    own = lax.dynamic_index_in_dim(gathered, source, 1, keepdims=False)
    partial_pre = jnp.dot(own, w_enc, preferred_element_type=jnp.float32)
    gates = masks.astype(jnp.float32)
    weights = w_dec[0]
    squares = flag * jnp.einsum("cd,cd->c", weights, weights, preferred_element_type=jnp.float32)
    term = flag * lax.dot_general(
        lax.all_gather(errors, "lat", axis=1, tiled=True)[0],
        weights,
        (((1,), (1,)), ((), ())),
        preferred_element_type=jnp.float32,
    )
    pre = lax.psum(partial_pre, "tgt") + b_enc[None, :]
    act = gates * pre
    dact, sumsq = lax.psum((term, squares), "tgt")
    grad = latent_grad(dact, sumsq, act, gates)
    grad_bias = jnp.sum(grad.astype(jnp.float32), axis=0)
    grad_enc = lax.dot_general(
        own, grad, (((0,), (0,)), ((), ())), preferred_element_type=jnp.float32
    )
    picker = (jnp.arange(S, dtype=jnp.int32) == source).astype(jnp.float32)
    part = lax.dot_general(
        grad, w_enc, (((1,), (1,)), ((), ())), preferred_element_type=jnp.float32
    )
    grad_in = lax.psum_scatter(
        part[:, None, :] * picker[None, :, None], "lat", scatter_dimension=0, tiled=True
    )
    return (grad_enc, grad_bias, grad_in)


def tile_grad(dact, sumsq, act, gates):
    norm = jnp.sqrt(sumsq)
    tanh_val = jnp.tanh(sharpness * act * norm)
    return gates * (dact + penalty * sharpness * norm * (1.0 - tanh_val * tanh_val))


def kernel(
    x_ref, we_hbm, b_ref, mask_hbm, wd_hbm, e_hbm, target_ref,
    g_out, own_out, bias_out, in_out,
    we, wd, mask, xs, es, xg, et, pre_send, pre_got, dact_send, dact_got,
    sq_send, sq_own, sq_got, pre_own, dact_own, g_own, g_got, acc_t,
    rs, rc, sums, ry, u, rz,
    load_sem, xz_s, xz_r, xy_s, xy_r, xc_s, xc_r, ez_s, ez_r, ey_s, ey_r, ec_s, ec_r,
    pre_s, pre_r, dact_s, dact_r, sq_s, sq_r, g_s, g_r, rs_s, rs_r, out_sem,
):
    f32 = jnp.float32
    me = lax.axis_index("lat")
    t = lax.axis_index("tgt")
    z, y, c = me // 4, (me // 2) % 2, me % 2
    source = z // (Z // S)
    half = NT * TILE
    far = [(z + k) % Z for k in range(Z)]
    near = [(z + Z - k) % Z for k in range(Z)]

    def lat_of(zz, yy, cc):
        return (zz * 2 + yy) * 2 + cc

    x_peer = (me, 1 - t)
    y_peer = (lat_of(z, 1 - y, c), t)
    c_peer = (lat_of(z, y, 1 - c), t)
    z_peer = [(lat_of(far[k], y, c), t) for k in range(Z)]

    def start_of(h):
        return (t if h == 0 else 1 - t) * half

    def we_load(h, j):
        at = pl.multiple_of(start_of(h) + j * TILE, TILE)
        return pltpu.make_async_copy(
            we_hbm.at[:, pl.ds(at, TILE)], we.at[h, j], load_sem.at[h * NT + j]
        )

    def wd_load(h):
        at = pl.multiple_of(start_of(h), half)
        return pltpu.make_async_copy(wd_hbm.at[0, pl.ds(at, half)], wd.at[h], load_sem.at[2 * NT + h])

    def mask_load(j):
        at = pl.multiple_of(start_of(0) + j * TILE, TILE)
        return pltpu.make_async_copy(
            mask_hbm.at[:, pl.ds(at, TILE)], mask.at[j], load_sem.at[2 * NT + 2 + j]
        )

    e_load = pltpu.make_async_copy(e_hbm.at[0], es.at[c, z * 2 + y], load_sem.at[3 * NT + 2])
    x_load = pltpu.make_async_copy(x_ref.at[source], xs.at[c, z * 2 + y], load_sem.at[3 * NT + 3])
    x_load.start()
    e_load.start()
    for h in (1, 0):
        for j in range(NT):
            we_load(h, j).start()
    wd_load(1).start()
    wd_load(0).start()
    for j in range(NT):
        mask_load(j).start()

    barrier = pltpu.get_barrier_semaphore()
    for peer in [x_peer, y_peer, c_peer] + z_peer[1:]:
        pl.semaphore_signal(barrier, inc=1, device_id=peer, device_id_type=MESH)
    pl.semaphore_wait(barrier, Z + 2)

    def remote(src, dst, send, recv, peer):
        return pltpu.make_async_remote_copy(
            src_ref=src, dst_ref=dst, send_sem=send, recv_sem=recv, device_id=peer, device_id_type=MESH
        )

    here = z * 2 + y
    xz = [
        remote(x_ref.at[far[k] // (Z // S)], xs.at[c, here], xz_s.at[k], xz_r.at[k], z_peer[k])
        for k in range(1, Z)
    ]
    ez = [remote(e_hbm.at[0], es.at[c, here], ez_s.at[k], ez_r.at[k], z_peer[k]) for k in range(1, Z)]
    for copy in xz + ez:
        copy.start()

    def along_y(buf, s, r):
        return [
            remote(buf.at[c, near[k] * 2 + y], buf.at[c, near[k] * 2 + y], s.at[k], r.at[k], y_peer)
            for k in range(Z)
        ]

    def along_c(buf, s, r):
        return [
            remote(
                buf.at[c, pl.ds(near[k] * 2, 2)], buf.at[c, pl.ds(near[k] * 2, 2)], s.at[k], r.at[k], c_peer
            )
            for k in range(Z)
        ]

    xy, xc = along_y(xs, xy_s, xy_r), along_c(xs, xc_s, xc_r)
    ey, ec = along_y(es, ey_s, ey_r), along_c(es, ec_s, ec_r)

    def z_to_y(load, along_z, y_copies):
        load.wait()
        y_copies[0].start()
        for k in range(1, Z):
            along_z[k - 1].wait_recv()
            y_copies[k].start()

    def y_to_c(y_copies, c_copies):
        for k in range(Z):
            y_copies[k].wait_recv()
            c_copies[k].start()

    def squares(h, out):
        @pl.loop(0, NT)
        def _(j):
            total = jnp.zeros((TILE, 128), f32)
            for at in range(0, wd.shape[2], 128):
                w = wd[h, pl.ds(pl.multiple_of(j * TILE, TILE), TILE), at : at + 128].astype(f32)
                total = total + w * w
            out[j] = flag * jnp.sum(total.T, axis=0, keepdims=True)

    flag = jnp.where(target_ref[t] >= source, 1.0, 0.0).astype(f32)

    z_to_y(x_load, xz, xy)
    wd_load(1).wait()
    y_to_c(xy, xc)
    z_to_y(e_load, ez, ey)
    for copy in xc:
        copy.wait_recv()
    for q in range(Z * 2):
        pair = jnp.concatenate([xs[0, q].astype(f32), xs[1, q].astype(f32)], axis=0)
        xg[q * 16 : q * 16 + 16] = pair.astype(jnp.bfloat16)

    for j in range(NT):
        we_load(1, j).wait()

    def pre_copy(j):
        return remote(pre_send.at[j], pre_got.at[j], pre_s.at[j], pre_r.at[j], x_peer)

    @pl.loop(0, NT)
    def _(j):
        part = jnp.dot(xg[...], we[1, j], preferred_element_type=f32)
        pre_send[j] = part.astype(jnp.bfloat16)
        pre_copy(j).start()

    y_to_c(ey, ec)
    squares(1, sq_send)
    sq_copy = remote(sq_send, sq_got, sq_s.at[0], sq_r.at[0], x_peer)
    sq_copy.start()
    for j in range(NT):
        we_load(0, j).wait()

    @pl.loop(0, NT)
    def _(j):
        pre_own[j] = jnp.dot(xg[...], we[0, j], preferred_element_type=f32)

    for copy in ec:
        copy.wait_recv()
    for q in range(0, Z * 2):
        pair = jnp.concatenate([es[0, q].astype(f32), es[1, q].astype(f32)], axis=0)
        et[q * 16 : q * 16 + 16] = pair.astype(jnp.bfloat16)

    def dact_tile(h, j):
        w = wd[h, pl.ds(pl.multiple_of(j * TILE, TILE), TILE)]
        return flag * lax.dot_general(
            et[...], w, (((1,), (1,)), ((), ())), preferred_element_type=f32
        )

    def dact_copy(j):
        return remote(dact_send.at[j], dact_got.at[j], dact_s.at[j], dact_r.at[j], x_peer)

    @pl.loop(0, NT)
    def _(j):
        dact_send[j] = dact_tile(1, j).astype(jnp.bfloat16)
        dact_copy(j).start()

    wd_load(0).wait()

    @pl.loop(0, NT)
    def _(j):
        dact_own[j] = dact_tile(0, j)

    squares(0, sq_own)
    sq_copy.wait_recv()
    for j in range(NT):
        mask_load(j).wait()

    def g_copy(j):
        return remote(g_own.at[j], g_got.at[j], g_s.at[j], g_r.at[j], x_peer)

    def input_part(w, grad):
        return jnp.dot(w, grad.T.astype(jnp.bfloat16), preferred_element_type=f32)

    acc_t[...] = jnp.zeros_like(acc_t)

    @pl.loop(0, NT)
    def _(j):
        pre_copy(j).wait_recv()
        dact_copy(j).wait_recv()
        at = pl.multiple_of(start_of(0) + j * TILE, TILE)
        gates = mask[j].astype(f32)
        pre = pre_own[j] + pre_got[j].astype(f32) + b_ref[:, pl.ds(at, TILE)]
        dact = dact_own[j] + dact_got[j].astype(f32)
        grad = tile_grad(dact, sq_own[j] + sq_got[j], gates * pre, gates).astype(jnp.bfloat16)
        g_own[j] = grad
        g_copy(j).start()
        grad = grad.astype(f32)
        bias_out[:, pl.ds(at, TILE)] = jnp.sum(grad, axis=0, keepdims=True)
        acc_t[...] += input_part(we[0, j], grad)

    def g_store(h, j):
        at = pl.multiple_of(start_of(h) + j * TILE, TILE)
        buf = g_own if h == 0 else g_got
        return pltpu.make_async_copy(buf.at[j], g_out.at[:, pl.ds(at, TILE)], out_sem.at[h * NT + j])

    own_store = pltpu.make_async_copy(xg, own_out, out_sem.at[2 * NT])
    own_store.start()
    for j in range(NT):
        g_store(0, j).start()

    @pl.loop(0, NT)
    def _(j):
        g_copy(j).wait_recv()
        g_store(1, j).start()
        at = pl.multiple_of(start_of(1) + j * TILE, TILE)
        grad = g_got[j].astype(f32)
        bias_out[:, pl.ds(at, TILE)] = jnp.sum(grad, axis=0, keepdims=True)
        acc_t[...] += input_part(we[1, j], grad)

    part = acc_t[...].T
    for zz in range(Z):
        for yy in range(2):
            for cc in range(2):
                b = lat_of(zz, yy, cc)
                rs[cc, yy, zz] = part[b * 8 : b * 8 + 8]
    to_c = remote(rs.at[1 - c], rc, rs_s.at[0], rs_r.at[0], c_peer)
    to_c.start()
    to_c.wait_recv()
    sums[...] = rs[c] + rc[...]
    to_y = remote(sums.at[1 - y], ry, rs_s.at[1], rs_r.at[1], y_peer)
    to_y.start()
    to_y.wait_recv()
    u[...] = sums[y] + ry[...]
    to_z = [
        remote(u.at[far[k]], rz.at[k], rs_s.at[1 + k], rs_r.at[1 + k], z_peer[k]) for k in range(1, Z)
    ]
    for copy in to_z:
        copy.start()
    terms = [u[z]]
    for k in range(1, Z):
        to_z[k - 1].wait_recv()
        terms.append(rz[k])
    for layer in range(S):
        total = jnp.zeros_like(terms[0])
        for k in range(Z):
            total = total + jnp.where(near[k] // (Z // S) == layer, terms[k], 0.0)
        in_out[layer] = total

    for copy in xz + ez + xy + xc + ey + ec + [sq_copy, to_c, to_y] + to_z:
        copy.wait_send()
    for j in range(NT):
        pre_copy(j).wait_send()
        dact_copy(j).wait_send()
        g_copy(j).wait_send()
        g_store(0, j).wait()
        g_store(1, j).wait()
    own_store.wait()


def local_kernel(inputs, w_enc, b_enc, masks, w_dec, errors, target_of):
    rows, _, width = inputs.shape
    tokens, block = masks.shape
    full = w_dec.shape[2]
    f32, bf16 = jnp.float32, jnp.bfloat16
    vmem = pltpu.VMEM
    dma = pltpu.SemaphoreType.DMA
    hbm, whole = pl.BlockSpec(memory_space=pl.ANY), pl.BlockSpec(memory_space=pltpu.VMEM)
    tiles = (NT, tokens, TILE)
    grad, own, bias, grad_in = pl.pallas_call(
        kernel,
        out_shape=(
            jax.ShapeDtypeStruct((tokens, block), bf16),
            jax.ShapeDtypeStruct((tokens, width), bf16),
            jax.ShapeDtypeStruct((1, block), f32),
            jax.ShapeDtypeStruct((S, rows, width), f32),
        ),
        in_specs=[hbm, hbm, whole, hbm, hbm, hbm, pl.BlockSpec(memory_space=pltpu.SMEM)],
        out_specs=(hbm, hbm, whole, whole),
        scratch_shapes=[
            vmem((2, NT, width, TILE), bf16),
            vmem((2, NT * TILE, full), bf16),
            vmem(tiles, jnp.int32),
            vmem((2, Z * 2, rows, width), bf16),
            vmem((2, Z * 2, rows, full), bf16),
            vmem((tokens, width), bf16),
            vmem((tokens, full), bf16),
            vmem(tiles, bf16), vmem(tiles, bf16), vmem(tiles, bf16), vmem(tiles, bf16),
            vmem((NT, 1, TILE), f32), vmem((NT, 1, TILE), f32), vmem((NT, 1, TILE), f32),
            vmem(tiles, f32), vmem(tiles, f32),
            vmem(tiles, bf16), vmem(tiles, bf16),
            vmem((width, tokens), f32),
            vmem((2, 2, Z, rows, width), f32),
            vmem((2, Z, rows, width), f32),
            vmem((2, Z, rows, width), f32),
            vmem((Z, rows, width), f32),
            vmem((Z, rows, width), f32),
            vmem((Z, rows, width), f32),
            dma((3 * NT + 4,)),
        ]
        + [dma((Z,))] * 12
        + [dma((NT,))] * 4
        + [dma((1,))] * 2
        + [dma((NT,))] * 2
        + [dma((Z + 1,))] * 2
        + [dma((2 * NT + 1,))],
        compiler_params=pltpu.CompilerParams(
            collective_id=0, has_side_effects=True, vmem_limit_bytes=48 * 1024 * 1024
        ),
    )(jnp.transpose(inputs, (1, 0, 2)), w_enc, b_enc[None, :], masks, w_dec, errors, target_of)
    grad_enc = lax.dot_general(own, grad, (((0,), (0,)), ((), ())), preferred_element_type=f32)
    return grad_enc, bias[0], jnp.transpose(grad_in, (1, 0, 2))


def solution(mesh):
    sizes = dict(mesh.shape)
    fits = sizes["lat"] == 4 * Z and sizes["tgt"] == 2
    return jax.shard_map(
        local_kernel if fits else local_any,
        mesh=mesh,
        in_specs=(
            P("lat", None, "tgt"),
            P("tgt", "lat"),
            P("lat"),
            P(None, "lat"),
            P("tgt", "lat", None),
            P("tgt", "lat", None),
            P(),
        ),
        out_specs=(P("tgt", "lat"), P("lat"), P("lat", None, "tgt")),
        check_vma=False,
    )
```

```python
import functools

import jax
import jax.numpy as jnp
from jax import lax
from jax.experimental import pallas as pl
from jax.experimental.pallas import tpu as pltpu
from jax.sharding import PartitionSpec as P

F = 16384
S = 2
MESH = pl.DeviceIdType.MESH
Z = 4
NT = 4
TILE = 256

penalty = 1.0
sharpness = 1.0


def latent_grad(dact, sumsq, act, gates):
    norm = jnp.sqrt(sumsq)[None, :]
    tanh_val = jnp.tanh(sharpness * act * norm)
    return (gates * (dact + penalty * sharpness * norm * (1.0 - tanh_val * tanh_val))).astype(
        jnp.bfloat16
    )


def local_any(inputs, w_enc, b_enc, masks, w_dec, errors, target_of):
    block = w_enc.shape[1]
    source = lax.axis_index("lat") * block // F
    slot = lax.axis_index("tgt")
    slots = jnp.arange(target_of.shape[0], dtype=jnp.int32)
    layer = jnp.sum(jnp.where(slots == slot, target_of, 0))
    flag = (layer >= source).astype(jnp.float32)
    gathered = lax.all_gather(inputs, "lat", axis=0, tiled=True)
    own = lax.dynamic_index_in_dim(gathered, source, 1, keepdims=False)
    partial_pre = jnp.dot(own, w_enc, preferred_element_type=jnp.float32)
    gates = masks.astype(jnp.float32)
    weights = w_dec[0]
    squares = flag * jnp.einsum("cd,cd->c", weights, weights, preferred_element_type=jnp.float32)
    term = flag * lax.dot_general(
        lax.all_gather(errors, "lat", axis=1, tiled=True)[0],
        weights,
        (((1,), (1,)), ((), ())),
        preferred_element_type=jnp.float32,
    )
    pre = lax.psum(partial_pre, "tgt") + b_enc[None, :]
    act = gates * pre
    dact, sumsq = lax.psum((term, squares), "tgt")
    grad = latent_grad(dact, sumsq, act, gates)
    grad_bias = jnp.sum(grad.astype(jnp.float32), axis=0)
    grad_enc = lax.dot_general(
        own, grad, (((0,), (0,)), ((), ())), preferred_element_type=jnp.float32
    )
    picker = (jnp.arange(S, dtype=jnp.int32) == source).astype(jnp.float32)
    part = lax.dot_general(
        grad, w_enc, (((1,), (1,)), ((), ())), preferred_element_type=jnp.float32
    )
    grad_in = lax.psum_scatter(
        part[:, None, :] * picker[None, :, None], "lat", scatter_dimension=0, tiled=True
    )
    return (grad_enc, grad_bias, grad_in)


CHUNKS = 3


def tile_grad(dact, sumsq, act, gates):
    norm = jnp.sqrt(sumsq)
    tanh_val = jnp.tanh(sharpness * act * norm)
    return gates * (dact + penalty * sharpness * norm * (1.0 - tanh_val * tanh_val))


def kernel(
    x_hbm, we_hbm, b_hbm, mask_hbm, wd_hbm, e_hbm, target_ref,
    g_out, own_out, in_out,
    we, wd, mask, b_ref, x_raw, x_in, xs, es, xg, own_t, eg, et, pre_send, pre_got, dact_send, dact_got,
    sq_send, sq_own, sq_got, pre_own, dact_own, g_own, g_got, acc_t,
    rs, rc, sums, ry, u, rz,
    load_sem, xz_s, xz_r, xy_s, xy_r, xc_s, xc_r, ez_s, ez_r, ey_s, ey_r, ec_s, ec_r,
    pre_s, pre_r, dact_s, dact_r, sq_s, sq_r, g_s, g_r, rc_s, rc_r, ry_s, ry_r, rz_s, rz_r, out_sem,
):
    f32 = jnp.float32
    me = lax.axis_index("lat")
    t = lax.axis_index("tgt")
    z, y, c = me // 4, (me // 2) % 2, me % 2
    source = z // (Z // S)
    half = NT * TILE
    far = [(z + k) % Z for k in range(Z)]
    near = [(z + Z - k) % Z for k in range(Z)]

    def lat_of(zz, yy, cc):
        return (zz * 2 + yy) * 2 + cc

    x_peer = (me, 1 - t)
    y_peer = (lat_of(z, 1 - y, c), t)
    c_peer = (lat_of(z, y, 1 - c), t)
    z_peer = [(lat_of(far[k], y, c), t) for k in range(Z)]

    def start_of(h):
        return (t if h == 0 else 1 - t) * half

    def we_load(h, j):
        at = pl.multiple_of(start_of(h) + j * TILE, TILE)
        return pltpu.make_async_copy(
            we_hbm.at[:, pl.ds(at, TILE)], we.at[h, j], load_sem.at[h * NT + j]
        )

    def wd_load(h, j):
        at = pl.multiple_of(start_of(h) + j * TILE, TILE)
        return pltpu.make_async_copy(
            wd_hbm.at[0, pl.ds(at, TILE)], wd.at[h, j], load_sem.at[(2 + h) * NT + j]
        )

    def mask_load(j):
        at = pl.multiple_of(start_of(0) + j * TILE, TILE)
        return pltpu.make_async_copy(
            mask_hbm.at[:, pl.ds(at, TILE)], mask.at[j], load_sem.at[4 * NT + j]
        )

    e_load = pltpu.make_async_copy(e_hbm.at[0], es.at[c, z * 2 + y], load_sem.at[5 * NT])
    x_load = pltpu.make_async_copy(x_hbm, x_raw, load_sem.at[5 * NT + 1])
    b_load = pltpu.make_async_copy(b_hbm, b_ref, load_sem.at[5 * NT + 2])
    x_load.start()
    e_load.start()
    for h in (1, 0):
        for j in range(NT):
            we_load(h, j).start()
        for j in range(NT):
            wd_load(h, j).start()
    b_load.start()
    for j in range(NT):
        mask_load(j).start()

    barrier = pltpu.get_barrier_semaphore()
    for peer in [x_peer, y_peer, c_peer] + z_peer[1:]:
        pl.semaphore_signal(barrier, inc=1, device_id=peer, device_id_type=MESH)
    x_load.wait()
    raw = x_raw[...].astype(f32)
    for layer in range(S):
        x_in[layer] = raw[:, layer, :].astype(jnp.bfloat16)
    xs[c, z * 2 + y] = x_in[source]
    pl.semaphore_wait(barrier, Z + 2)

    def remote(src, dst, send, recv, peer):
        return pltpu.make_async_remote_copy(
            src_ref=src, dst_ref=dst, send_sem=send, recv_sem=recv, device_id=peer, device_id_type=MESH
        )

    here = z * 2 + y
    xz = [
        remote(x_in.at[far[k] // (Z // S)], xs.at[c, here], xz_s.at[k], xz_r.at[k], z_peer[k])
        for k in range(1, Z)
    ]
    ez = [remote(e_hbm.at[0], es.at[c, here], ez_s.at[k], ez_r.at[k], z_peer[k]) for k in range(1, Z)]
    for copy in xz + ez:
        copy.start()

    def along_y(buf, s, r):
        return [
            remote(buf.at[c, near[k] * 2 + y], buf.at[c, near[k] * 2 + y], s.at[k], r.at[k], y_peer)
            for k in range(Z)
        ]

    def along_c(buf, s, r):
        return [
            remote(
                buf.at[c, pl.ds(near[k] * 2, 2)], buf.at[c, pl.ds(near[k] * 2, 2)], s.at[k], r.at[k], c_peer
            )
            for k in range(Z)
        ]

    xy, xc = along_y(xs, xy_s, xy_r), along_c(xs, xc_s, xc_r)
    ey, ec = along_y(es, ey_s, ey_r), along_c(es, ec_s, ec_r)

    def z_to_y(along_z, y_copies):
        y_copies[0].start()
        for k in range(1, Z):
            along_z[k - 1].wait_recv()
            y_copies[k].start()

    def y_to_c(y_copies, c_copies):
        for k in range(Z):
            y_copies[k].wait_recv()
            c_copies[k].start()

    def squares(h, j, out):
        wd_load(h, j).wait()
        total = jnp.zeros((TILE, 128), f32)
        for at in range(0, wd.shape[3], 128):
            w = wd[h, j, :, at : at + 128].astype(f32)
            total = total + w * w
        out[j] = flag * jnp.sum(total.T, axis=0, keepdims=True)

    flag = jnp.where(target_ref[t] >= source, 1.0, 0.0).astype(f32)

    z_to_y(xz, xy)
    squares(1, 0, sq_send)
    y_to_c(xy, xc)
    squares(1, 1, sq_send)
    e_load.wait()
    z_to_y(ez, ey)
    pl.loop(2, NT)(lambda j: squares(1, j, sq_send))
    for copy in xc:
        copy.wait_recv()
    for q in range(Z * 2):
        pair = jnp.concatenate([xs[0, q].astype(f32), xs[1, q].astype(f32)], axis=0)
        xg[q * 16 : q * 16 + 16] = pair.astype(jnp.bfloat16)

    for j in range(NT):
        we_load(1, j).wait()

    def pre_copy(j):
        return remote(pre_send.at[j], pre_got.at[j], pre_s.at[j], pre_r.at[j], x_peer)

    @pl.loop(0, NT)
    def _(j):
        part = jnp.dot(xg[...], we[1, j], preferred_element_type=f32)
        pre_send[j] = part.astype(jnp.bfloat16)
        pre_copy(j).start()

    y_to_c(ey, ec)
    sq_copy = remote(sq_send, sq_got, sq_s.at[0], sq_r.at[0], x_peer)
    sq_copy.start()
    for j in range(NT):
        we_load(0, j).wait()

    @pl.loop(0, NT)
    def _(j):
        pre_own[j] = jnp.dot(xg[...], we[0, j], preferred_element_type=f32)

    pl.loop(0, NT)(lambda j: squares(0, j, sq_own))
    for at in range(0, xg.shape[1], 128):
        own_t[at : at + 128] = xg[:, at : at + 128].astype(f32).T.astype(jnp.bfloat16)
    own_store = pltpu.make_async_copy(own_t, own_out, out_sem.at[2 * NT])
    own_store.start()
    for copy in ec:
        copy.wait_recv()
    for q in range(0, Z * 2):
        pair = jnp.concatenate([es[0, q].astype(f32), es[1, q].astype(f32)], axis=0)
        eg[q * 16 : q * 16 + 16] = pair.astype(jnp.bfloat16)
    for at in range(0, eg.shape[1], 128):
        et[at : at + 128] = eg[:, at : at + 128].astype(f32).T.astype(jnp.bfloat16)

    def dact_tile(h, j):
        return flag * jnp.dot(wd[h, j], et[...], preferred_element_type=f32).T

    def dact_copy(j):
        return remote(dact_send.at[j], dact_got.at[j], dact_s.at[j], dact_r.at[j], x_peer)

    @pl.loop(0, NT)
    def _(j):
        dact_send[j] = dact_tile(1, j).astype(jnp.bfloat16)
        dact_copy(j).start()

    @pl.loop(0, NT)
    def _(j):
        dact_own[j] = dact_tile(0, j)

    b_load.wait()
    sq_copy.wait_recv()
    for j in range(NT):
        mask_load(j).wait()

    def g_copy(j):
        return remote(g_own.at[j], g_got.at[j], g_s.at[j], g_r.at[j], x_peer)

    def input_part(w, grad):
        return jnp.dot(w, grad.T.astype(jnp.bfloat16), preferred_element_type=f32)

    acc_t[...] = jnp.zeros_like(acc_t)

    @pl.loop(0, NT)
    def _(j):
        pre_copy(j).wait_recv()
        dact_copy(j).wait_recv()
        at = pl.multiple_of(start_of(0) + j * TILE, TILE)
        gates = mask[j].astype(f32)
        pre = pre_own[j] + pre_got[j].astype(f32) + b_ref[:, pl.ds(at, TILE)]
        dact = dact_own[j] + dact_got[j].astype(f32)
        grad = tile_grad(dact, sq_own[j] + sq_got[j], gates * pre, gates).astype(jnp.bfloat16)
        g_own[j] = grad
        g_copy(j).start()
        grad = grad.astype(f32)
        acc_t[...] += input_part(we[0, j], grad)

    def g_store(h, j):
        at = pl.multiple_of(start_of(h) + j * TILE, TILE)
        buf = g_own if h == 0 else g_got
        return pltpu.make_async_copy(buf.at[j], g_out.at[:, pl.ds(at, TILE)], out_sem.at[h * NT + j])

    for j in range(NT):
        g_store(0, j).start()

    @pl.loop(0, NT - 1)
    def _(j):
        g_copy(j).wait_recv()
        g_store(1, j).start()
        acc_t[...] += input_part(we[1, j], g_got[j].astype(f32))

    g_copy(NT - 1).wait_recv()
    g_store(1, NT - 1).start()
    last = g_got[NT - 1].astype(f32)
    chunks = range(rs.shape[0])
    wide = rs.shape[-1]
    to_c = [remote(rs.at[d, 1 - c], rc.at[d], rc_s.at[d], rc_r.at[d], c_peer) for d in chunks]
    to_y = [remote(sums.at[d, 1 - y], ry.at[d], ry_s.at[d], ry_r.at[d], y_peer) for d in chunks]
    to_z = [
        remote(
            u.at[d, far[k]], rz.at[d, k], rz_s.at[d * Z + k], rz_r.at[d * Z + k], z_peer[k]
        )
        for d in chunks
        for k in range(1, Z)
    ]
    for d in chunks:
        at = d * wide
        part = (acc_t[at : at + wide] + input_part(we[1, NT - 1, at : at + wide], last)).T
        for zz in range(Z):
            for yy in range(2):
                for cc in range(2):
                    b = lat_of(zz, yy, cc)
                    rs[d, cc, yy, zz] = part[b * 8 : b * 8 + 8]
        to_c[d].start()
    for d in chunks:
        to_c[d].wait_recv()
        sums[d, 1 - y] = (rs[d, c, 1 - y] + rc[d, 1 - y]).astype(jnp.bfloat16)
        to_y[d].start()
        u[d] = rs[d, c, y] + rc[d, y]
    for d in chunks:
        to_y[d].wait_recv()
        u[d] = u[d] + ry[d].astype(f32)
        for copy in to_z[d * (Z - 1) : (d + 1) * (Z - 1)]:
            copy.start()
    for d in chunks:
        terms = [u[d, z]]
        for k in range(1, Z):
            to_z[d * (Z - 1) + k - 1].wait_recv()
            terms.append(rz[d, k])
        for layer in range(S):
            total = jnp.zeros_like(terms[0])
            for k in range(Z):
                total = total + jnp.where(near[k] // (Z // S) == layer, terms[k], 0.0)
            in_out[layer, :, d * wide : (d + 1) * wide] = total

    for copy in xz + ez + xy + xc + ey + ec + [sq_copy] + to_c + to_y + to_z:
        copy.wait_send()
    for j in range(NT):
        pre_copy(j).wait_send()
        dact_copy(j).wait_send()
        g_copy(j).wait_send()
        g_store(0, j).wait()
        g_store(1, j).wait()
    own_store.wait()


def encoder_kernel(own_ref, g_ref, in_ref, enc_out, bias_out, in_out):
    @pl.when(pl.program_id(0) == 0)
    def _():
        bias_out[...] = jnp.sum(g_ref[...].astype(jnp.float32), axis=0, keepdims=True)
        for layer in range(S):
            in_out[:, layer, :] = in_ref[layer]

    enc_out[...] = jnp.dot(own_ref[...], g_ref[...], preferred_element_type=jnp.float32)


def local_kernel(inputs, w_enc, b_enc, masks, w_dec, errors, target_of):
    rows, _, width = inputs.shape
    tokens, block = masks.shape
    full = w_dec.shape[2]
    f32, bf16 = jnp.float32, jnp.bfloat16
    vmem = pltpu.VMEM
    dma = pltpu.SemaphoreType.DMA
    hbm = pl.BlockSpec(memory_space=pltpu.HBM)
    free, whole = pl.BlockSpec(memory_space=pl.ANY), pl.BlockSpec(memory_space=pltpu.VMEM)
    tiles = (NT, tokens, TILE)
    wide = width // CHUNKS
    grad, own_t, grad_in = pl.pallas_call(
        kernel,
        out_shape=(
            jax.ShapeDtypeStruct((tokens, block), bf16),
            jax.ShapeDtypeStruct((width, tokens), bf16),
            jax.ShapeDtypeStruct((S, rows, width), f32),
        ),
        in_specs=[hbm] * 6 + [pl.BlockSpec(memory_space=pltpu.SMEM)],
        out_specs=(free, free, whole),
        scratch_shapes=[
            vmem((2, NT, width, TILE), bf16),
            vmem((2, NT, TILE, full), bf16),
            vmem(tiles, jnp.int32),
            vmem((1, block), f32),
            vmem((rows, S, width), bf16),
            vmem((S, rows, width), bf16),
            vmem((2, Z * 2, rows, width), bf16),
            vmem((2, Z * 2, rows, full), bf16),
            vmem((tokens, width), bf16),
            vmem((width, tokens), bf16),
            vmem((tokens, full), bf16),
            vmem((full, tokens), bf16),
            vmem(tiles, bf16), vmem(tiles, bf16), vmem(tiles, bf16), vmem(tiles, bf16),
            vmem((NT, 1, TILE), f32), vmem((NT, 1, TILE), f32), vmem((NT, 1, TILE), f32),
            vmem(tiles, f32), vmem(tiles, f32),
            vmem(tiles, bf16), vmem(tiles, bf16),
            vmem((width, tokens), f32),
            vmem((CHUNKS, 2, 2, Z, rows, wide), f32),
            vmem((CHUNKS, 2, Z, rows, wide), f32),
            vmem((CHUNKS, 2, Z, rows, wide), bf16),
            vmem((CHUNKS, Z, rows, wide), bf16),
            vmem((CHUNKS, Z, rows, wide), f32),
            vmem((CHUNKS, Z, rows, wide), f32),
            dma((5 * NT + 3,)),
        ]
        + [dma((Z,))] * 12
        + [dma((NT,))] * 4
        + [dma((1,))] * 2
        + [dma((NT,))] * 2
        + [dma((CHUNKS,))] * 4
        + [dma((CHUNKS * Z,))] * 2
        + [dma((2 * NT + 1,))],
        compiler_params=pltpu.CompilerParams(
            collective_id=0, has_side_effects=True, vmem_limit_bytes=62 * 1024 * 1024
        ),
    )(inputs, w_enc, b_enc[None, :], masks, w_dec, errors, target_of)
    step = width // 6
    grad_enc, bias, grad_in = pl.pallas_call(
        encoder_kernel,
        grid=(width // step,),
        out_shape=(
            jax.ShapeDtypeStruct((width, block), f32),
            jax.ShapeDtypeStruct((1, block), f32),
            jax.ShapeDtypeStruct((rows, S, width), f32),
        ),
        in_specs=[
            pl.BlockSpec((step, tokens), lambda i: (i, 0)),
            pl.BlockSpec((tokens, block), lambda i: (0, 0)),
            pl.BlockSpec((S, rows, width), lambda i: (0, 0, 0)),
        ],
        out_specs=(
            pl.BlockSpec((step, block), lambda i: (i, 0)),
            pl.BlockSpec((1, block), lambda i: (0, 0)),
            pl.BlockSpec((rows, S, width), lambda i: (0, 0, 0)),
        ),
        compiler_params=pltpu.CompilerParams(vmem_limit_bytes=62 * 1024 * 1024),
    )(own_t, grad, grad_in)
    return grad_enc, bias[0], grad_in


def solution(mesh):
    sizes = dict(mesh.shape)
    fits = sizes["lat"] == 4 * Z and sizes["tgt"] == 2
    return jax.shard_map(
        local_kernel if fits else local_any,
        mesh=mesh,
        in_specs=(
            P("lat", None, "tgt"),
            P("tgt", "lat"),
            P("lat"),
            P(None, "lat"),
            P("tgt", "lat", None),
            P("tgt", "lat", None),
            P(),
        ),
        out_specs=(P("tgt", "lat"), P("lat"), P("lat", None, "tgt")),
        check_vma=False,
    )
```

```python
import functools

import jax
import jax.numpy as jnp
from jax import lax
from jax.experimental import pallas as pl
from jax.experimental.pallas import tpu as pltpu
from jax.sharding import PartitionSpec as P

F = 16384
S = 2
MESH = pl.DeviceIdType.MESH
Z = 4
NT = 4
TILE = 256

penalty = 1.0
sharpness = 1.0


def latent_grad(dact, sumsq, act, gates):
    norm = jnp.sqrt(sumsq)[None, :]
    tanh_val = jnp.tanh(sharpness * act * norm)
    return (gates * (dact + penalty * sharpness * norm * (1.0 - tanh_val * tanh_val))).astype(
        jnp.bfloat16
    )


def local_any(inputs, w_enc, b_enc, masks, w_dec, errors, target_of):
    block = w_enc.shape[1]
    source = lax.axis_index("lat") * block // F
    slot = lax.axis_index("tgt")
    slots = jnp.arange(target_of.shape[0], dtype=jnp.int32)
    layer = jnp.sum(jnp.where(slots == slot, target_of, 0))
    flag = (layer >= source).astype(jnp.float32)
    gathered = lax.all_gather(inputs, "lat", axis=0, tiled=True)
    own = lax.dynamic_index_in_dim(gathered, source, 1, keepdims=False)
    partial_pre = jnp.dot(own, w_enc, preferred_element_type=jnp.float32)
    gates = masks.astype(jnp.float32)
    weights = w_dec[0]
    squares = flag * jnp.einsum("cd,cd->c", weights, weights, preferred_element_type=jnp.float32)
    term = flag * lax.dot_general(
        lax.all_gather(errors, "lat", axis=1, tiled=True)[0],
        weights,
        (((1,), (1,)), ((), ())),
        preferred_element_type=jnp.float32,
    )
    pre = lax.psum(partial_pre, "tgt") + b_enc[None, :]
    act = gates * pre
    dact, sumsq = lax.psum((term, squares), "tgt")
    grad = latent_grad(dact, sumsq, act, gates)
    grad_bias = jnp.sum(grad.astype(jnp.float32), axis=0)
    grad_enc = lax.dot_general(
        own, grad, (((0,), (0,)), ((), ())), preferred_element_type=jnp.float32
    )
    picker = (jnp.arange(S, dtype=jnp.int32) == source).astype(jnp.float32)
    part = lax.dot_general(
        grad, w_enc, (((1,), (1,)), ((), ())), preferred_element_type=jnp.float32
    )
    grad_in = lax.psum_scatter(
        part[:, None, :] * picker[None, :, None], "lat", scatter_dimension=0, tiled=True
    )
    return (grad_enc, grad_bias, grad_in)


CHUNKS = 3


def tile_grad(dact, sumsq, act, gates):
    norm = jnp.sqrt(sumsq)
    tanh_val = jnp.tanh(sharpness * act * norm)
    return gates * (dact + penalty * sharpness * norm * (1.0 - tanh_val * tanh_val))


def kernel(
    x_hbm, we_hbm, b_hbm, mask_hbm, wd_hbm, e_hbm, target_ref,
    g_out, own_out, in_out,
    we, wd, mask, b_ref, x_raw, x_in, xs, es, xg, own_t, eg, et, pre_send, pre_got, dact_send, dact_got,
    sq_send, sq_own, sq_got, pre_own, dact_own, g_own, g_got, acc_t,
    rs, rc, sums, ry, u, rz,
    load_sem, xz_s, xz_r, xy_s, xy_r, xc_s, xc_r, ez_s, ez_r, ey_s, ey_r, ec_s, ec_r,
    pre_s, pre_r, dact_s, dact_r, sq_s, sq_r, g_s, g_r, rc_s, rc_r, ry_s, ry_r, rz_s, rz_r, out_sem,
):
    f32 = jnp.float32
    me = lax.axis_index("lat")
    t = lax.axis_index("tgt")
    z, y, c = me // 4, (me // 2) % 2, me % 2
    source = z // (Z // S)
    half = NT * TILE
    far = [(z + k) % Z for k in range(Z)]
    near = [(z + Z - k) % Z for k in range(Z)]

    def lat_of(zz, yy, cc):
        return (zz * 2 + yy) * 2 + cc

    x_peer = (me, 1 - t)
    y_peer = (lat_of(z, 1 - y, c), t)
    c_peer = (lat_of(z, y, 1 - c), t)
    z_peer = [(lat_of(far[k], y, c), t) for k in range(Z)]

    def start_of(h):
        return (t if h == 0 else 1 - t) * half

    def we_load(h, j):
        at = pl.multiple_of(start_of(h) + j * TILE, TILE)
        return pltpu.make_async_copy(
            we_hbm.at[:, pl.ds(at, TILE)], we.at[h, j], load_sem.at[h * NT + j]
        )

    def wd_load(h, j):
        at = pl.multiple_of(start_of(h) + j * TILE, TILE)
        return pltpu.make_async_copy(
            wd_hbm.at[0, pl.ds(at, TILE)], wd.at[h, j], load_sem.at[(2 + h) * NT + j]
        )

    def mask_load(j):
        at = pl.multiple_of(start_of(0) + j * TILE, TILE)
        return pltpu.make_async_copy(
            mask_hbm.at[:, pl.ds(at, TILE)], mask.at[j], load_sem.at[4 * NT + j]
        )

    e_load = pltpu.make_async_copy(e_hbm.at[0], es.at[c, z * 2 + y], load_sem.at[5 * NT])
    x_load = pltpu.make_async_copy(x_hbm, x_raw, load_sem.at[5 * NT + 1])
    b_load = pltpu.make_async_copy(b_hbm, b_ref, load_sem.at[5 * NT + 2])
    x_load.start()
    e_load.start()
    for j in range(2):
        wd_load(1, j).start()
    for j in range(NT):
        we_load(1, j).start()

    barrier = pltpu.get_barrier_semaphore()
    for peer in [x_peer, y_peer, c_peer] + z_peer[1:]:
        pl.semaphore_signal(barrier, inc=1, device_id=peer, device_id_type=MESH)
    x_load.wait()
    raw = x_raw[...].astype(f32)
    for layer in range(S):
        x_in[layer] = raw[:, layer, :].astype(jnp.bfloat16)
    xs[c, z * 2 + y] = x_in[source]
    pl.semaphore_wait(barrier, Z + 2)

    def remote(src, dst, send, recv, peer):
        return pltpu.make_async_remote_copy(
            src_ref=src, dst_ref=dst, send_sem=send, recv_sem=recv, device_id=peer, device_id_type=MESH
        )

    here = z * 2 + y
    xz = [
        remote(x_in.at[far[k] // (Z // S)], xs.at[c, here], xz_s.at[k], xz_r.at[k], z_peer[k])
        for k in range(1, Z)
    ]
    ez = [remote(e_hbm.at[0], es.at[c, here], ez_s.at[k], ez_r.at[k], z_peer[k]) for k in range(1, Z)]
    for copy in xz + ez:
        copy.start()
    for j in range(2, NT):
        wd_load(1, j).start()

    def along_y(buf, s, r):
        return [
            remote(buf.at[c, near[k] * 2 + y], buf.at[c, near[k] * 2 + y], s.at[k], r.at[k], y_peer)
            for k in range(Z)
        ]

    def along_c(buf, s, r):
        return [
            remote(
                buf.at[c, pl.ds(near[k] * 2, 2)], buf.at[c, pl.ds(near[k] * 2, 2)], s.at[k], r.at[k], c_peer
            )
            for k in range(Z)
        ]

    xy, xc = along_y(xs, xy_s, xy_r), along_c(xs, xc_s, xc_r)
    ey, ec = along_y(es, ey_s, ey_r), along_c(es, ec_s, ec_r)

    def z_to_y(along_z, y_copies):
        y_copies[0].start()
        for k in range(1, Z):
            along_z[k - 1].wait_recv()
            y_copies[k].start()

    def y_to_c(y_copies, c_copies):
        for k in range(Z):
            y_copies[k].wait_recv()
            c_copies[k].start()

    def squares(h, j, out):
        wd_load(h, j).wait()
        total = jnp.zeros((TILE, 128), f32)
        for at in range(0, wd.shape[3], 128):
            w = wd[h, j, :, at : at + 128].astype(f32)
            total = total + w * w
        out[j] = flag * jnp.sum(total.T, axis=0, keepdims=True)

    flag = jnp.where(target_ref[t] >= source, 1.0, 0.0).astype(f32)

    z_to_y(xz, xy)
    squares(1, 0, sq_send)
    y_to_c(xy, xc)
    for j in range(NT):
        we_load(0, j).start()
    squares(1, 1, sq_send)
    e_load.wait()
    z_to_y(ez, ey)
    for j in range(NT):
        wd_load(0, j).start()
        mask_load(j).start()
    b_load.start()
    pl.loop(2, NT)(lambda j: squares(1, j, sq_send))
    for copy in xc:
        copy.wait_recv()
    for q in range(Z * 2):
        pair = jnp.concatenate([xs[0, q].astype(f32), xs[1, q].astype(f32)], axis=0)
        xg[q * 16 : q * 16 + 16] = pair.astype(jnp.bfloat16)

    for j in range(NT):
        we_load(1, j).wait()

    def pre_copy(j):
        return remote(pre_send.at[j], pre_got.at[j], pre_s.at[j], pre_r.at[j], x_peer)

    @pl.loop(0, NT)
    def _(j):
        part = jnp.dot(xg[...], we[1, j], preferred_element_type=f32)
        pre_send[j] = part.astype(jnp.bfloat16)
        pre_copy(j).start()

    y_to_c(ey, ec)
    sq_copy = remote(sq_send, sq_got, sq_s.at[0], sq_r.at[0], x_peer)
    sq_copy.start()
    for j in range(NT):
        we_load(0, j).wait()

    @pl.loop(0, NT)
    def _(j):
        pre_own[j] = jnp.dot(xg[...], we[0, j], preferred_element_type=f32)

    pl.loop(0, NT)(lambda j: squares(0, j, sq_own))
    for at in range(0, xg.shape[1], 128):
        own_t[at : at + 128] = xg[:, at : at + 128].astype(f32).T.astype(jnp.bfloat16)
    own_store = pltpu.make_async_copy(own_t, own_out, out_sem.at[2 * NT])
    own_store.start()
    for copy in ec:
        copy.wait_recv()
    for q in range(0, Z * 2):
        pair = jnp.concatenate([es[0, q].astype(f32), es[1, q].astype(f32)], axis=0)
        eg[q * 16 : q * 16 + 16] = pair.astype(jnp.bfloat16)
    for at in range(0, eg.shape[1], 128):
        et[at : at + 128] = eg[:, at : at + 128].astype(f32).T.astype(jnp.bfloat16)

    def dact_tile(h, j):
        return flag * jnp.dot(wd[h, j], et[...], preferred_element_type=f32).T

    def dact_copy(j):
        return remote(dact_send.at[j], dact_got.at[j], dact_s.at[j], dact_r.at[j], x_peer)

    @pl.loop(0, NT)
    def _(j):
        dact_send[j] = dact_tile(1, j).astype(jnp.bfloat16)
        dact_copy(j).start()

    @pl.loop(0, NT)
    def _(j):
        dact_own[j] = dact_tile(0, j)

    b_load.wait()
    sq_copy.wait_recv()
    for j in range(NT):
        mask_load(j).wait()

    def g_copy(j):
        return remote(g_own.at[j], g_got.at[j], g_s.at[j], g_r.at[j], x_peer)

    def input_part(w, grad):
        return jnp.dot(w, grad.T.astype(jnp.bfloat16), preferred_element_type=f32)

    acc_t[...] = jnp.zeros_like(acc_t)

    @pl.loop(0, NT)
    def _(j):
        pre_copy(j).wait_recv()
        dact_copy(j).wait_recv()
        at = pl.multiple_of(start_of(0) + j * TILE, TILE)
        gates = mask[j].astype(f32)
        pre = pre_own[j] + pre_got[j].astype(f32) + b_ref[:, pl.ds(at, TILE)]
        dact = dact_own[j] + dact_got[j].astype(f32)
        grad = tile_grad(dact, sq_own[j] + sq_got[j], gates * pre, gates).astype(jnp.bfloat16)
        g_own[j] = grad
        g_copy(j).start()
        grad = grad.astype(f32)
        acc_t[...] += input_part(we[0, j], grad)

    def g_store(h, j):
        at = pl.multiple_of(start_of(h) + j * TILE, TILE)
        buf = g_own if h == 0 else g_got
        return pltpu.make_async_copy(buf.at[j], g_out.at[:, pl.ds(at, TILE)], out_sem.at[h * NT + j])

    for j in range(NT):
        g_store(0, j).start()

    @pl.loop(0, NT - 1)
    def _(j):
        g_copy(j).wait_recv()
        g_store(1, j).start()
        acc_t[...] += input_part(we[1, j], g_got[j].astype(f32))

    g_copy(NT - 1).wait_recv()
    g_store(1, NT - 1).start()
    last = g_got[NT - 1].astype(f32)
    chunks = range(rs.shape[0])
    wide = rs.shape[-1]
    to_c = [remote(rs.at[d, 1 - c], rc.at[d], rc_s.at[d], rc_r.at[d], c_peer) for d in chunks]
    to_y = [remote(sums.at[d, 1 - y], ry.at[d], ry_s.at[d], ry_r.at[d], y_peer) for d in chunks]
    to_z = [
        remote(
            u.at[d, far[k]], rz.at[d, k], rz_s.at[d * Z + k], rz_r.at[d * Z + k], z_peer[k]
        )
        for d in chunks
        for k in range(1, Z)
    ]
    for d in chunks:
        at = d * wide
        part = (acc_t[at : at + wide] + input_part(we[1, NT - 1, at : at + wide], last)).T
        for zz in range(Z):
            for yy in range(2):
                for cc in range(2):
                    b = lat_of(zz, yy, cc)
                    rs[d, cc, yy, zz] = part[b * 8 : b * 8 + 8]
        to_c[d].start()
    for d in chunks:
        to_c[d].wait_recv()
        sums[d, 1 - y] = (rs[d, c, 1 - y] + rc[d, 1 - y]).astype(jnp.bfloat16)
        to_y[d].start()
        u[d] = rs[d, c, y] + rc[d, y]
    for d in chunks:
        to_y[d].wait_recv()
        u[d] = u[d] + ry[d].astype(f32)
        for copy in to_z[d * (Z - 1) : (d + 1) * (Z - 1)]:
            copy.start()
    for d in chunks:
        terms = [u[d, z]]
        for k in range(1, Z):
            to_z[d * (Z - 1) + k - 1].wait_recv()
            terms.append(rz[d, k])
        for layer in range(S):
            total = jnp.zeros_like(terms[0])
            for k in range(Z):
                total = total + jnp.where(near[k] // (Z // S) == layer, terms[k], 0.0)
            in_out[layer, :, d * wide : (d + 1) * wide] = total

    for copy in xz + ez + xy + xc + ey + ec + [sq_copy] + to_c + to_y + to_z:
        copy.wait_send()
    for j in range(NT):
        pre_copy(j).wait_send()
        dact_copy(j).wait_send()
        g_copy(j).wait_send()
        g_store(0, j).wait()
        g_store(1, j).wait()
    own_store.wait()


def encoder_kernel(own_ref, g_ref, in_ref, enc_out, bias_out, in_out):
    bias_out[...] = jnp.sum(g_ref[...].astype(jnp.float32), axis=0, keepdims=True)

    @pl.when(pl.program_id(0) == 0)
    def _():
        for layer in range(S):
            in_out[:, layer, :] = in_ref[layer]

    enc_out[...] = jnp.dot(own_ref[...], g_ref[...], preferred_element_type=jnp.float32)


def local_kernel(inputs, w_enc, b_enc, masks, w_dec, errors, target_of):
    rows, _, width = inputs.shape
    tokens, block = masks.shape
    full = w_dec.shape[2]
    f32, bf16 = jnp.float32, jnp.bfloat16
    vmem = pltpu.VMEM
    dma = pltpu.SemaphoreType.DMA
    hbm = pl.BlockSpec(memory_space=pltpu.HBM)
    free, whole = pl.BlockSpec(memory_space=pl.ANY), pl.BlockSpec(memory_space=pltpu.VMEM)
    tiles = (NT, tokens, TILE)
    wide = width // CHUNKS
    grad, own_t, grad_in = pl.pallas_call(
        kernel,
        out_shape=(
            jax.ShapeDtypeStruct((tokens, block), bf16),
            jax.ShapeDtypeStruct((width, tokens), bf16),
            jax.ShapeDtypeStruct((S, rows, width), f32),
        ),
        in_specs=[hbm] * 6 + [pl.BlockSpec(memory_space=pltpu.SMEM)],
        out_specs=(free, free, whole),
        scratch_shapes=[
            vmem((2, NT, width, TILE), bf16),
            vmem((2, NT, TILE, full), bf16),
            vmem(tiles, jnp.int32),
            vmem((1, block), f32),
            vmem((rows, S, width), bf16),
            vmem((S, rows, width), bf16),
            vmem((2, Z * 2, rows, width), bf16),
            vmem((2, Z * 2, rows, full), bf16),
            vmem((tokens, width), bf16),
            vmem((width, tokens), bf16),
            vmem((tokens, full), bf16),
            vmem((full, tokens), bf16),
            vmem(tiles, bf16), vmem(tiles, bf16), vmem(tiles, bf16), vmem(tiles, bf16),
            vmem((NT, 1, TILE), f32), vmem((NT, 1, TILE), f32), vmem((NT, 1, TILE), f32),
            vmem(tiles, f32), vmem(tiles, f32),
            vmem(tiles, bf16), vmem(tiles, bf16),
            vmem((width, tokens), f32),
            vmem((CHUNKS, 2, 2, Z, rows, wide), f32),
            vmem((CHUNKS, 2, Z, rows, wide), f32),
            vmem((CHUNKS, 2, Z, rows, wide), bf16),
            vmem((CHUNKS, Z, rows, wide), bf16),
            vmem((CHUNKS, Z, rows, wide), f32),
            vmem((CHUNKS, Z, rows, wide), f32),
            dma((5 * NT + 3,)),
        ]
        + [dma((Z,))] * 12
        + [dma((NT,))] * 4
        + [dma((1,))] * 2
        + [dma((NT,))] * 2
        + [dma((CHUNKS,))] * 4
        + [dma((CHUNKS * Z,))] * 2
        + [dma((2 * NT + 1,))],
        compiler_params=pltpu.CompilerParams(
            collective_id=0, has_side_effects=True, vmem_limit_bytes=62 * 1024 * 1024
        ),
    )(inputs, w_enc, b_enc[None, :], masks, w_dec, errors, target_of)
    grad_enc, bias, grad_in = pl.pallas_call(
        encoder_kernel,
        grid=(block // TILE,),
        out_shape=(
            jax.ShapeDtypeStruct((width, block), f32),
            jax.ShapeDtypeStruct((1, block), f32),
            jax.ShapeDtypeStruct((rows, S, width), f32),
        ),
        in_specs=[
            pl.BlockSpec((width, tokens), lambda i: (0, 0)),
            pl.BlockSpec((tokens, TILE), lambda i: (0, i)),
            pl.BlockSpec((S, rows, width), lambda i: (0, 0, 0)),
        ],
        out_specs=(
            pl.BlockSpec((width, TILE), lambda i: (0, i)),
            pl.BlockSpec((1, TILE), lambda i: (0, i)),
            pl.BlockSpec((rows, S, width), lambda i: (0, 0, 0)),
        ),
        compiler_params=pltpu.CompilerParams(vmem_limit_bytes=62 * 1024 * 1024),
    )(own_t, grad, grad_in)
    return grad_enc, bias[0], grad_in


def solution(mesh):
    sizes = dict(mesh.shape)
    fits = sizes["lat"] == 4 * Z and sizes["tgt"] == 2
    return jax.shard_map(
        local_kernel if fits else local_any,
        mesh=mesh,
        in_specs=(
            P("lat", None, "tgt"),
            P("tgt", "lat"),
            P("lat"),
            P(None, "lat"),
            P("tgt", "lat", None),
            P("tgt", "lat", None),
            P(),
        ),
        out_specs=(P("tgt", "lat"), P("lat"), P("lat", None, "tgt")),
        check_vma=False,
    )
```

```python
import functools

import jax
import jax.numpy as jnp
from jax import lax
from jax.experimental import pallas as pl
from jax.experimental.pallas import tpu as pltpu
from jax.sharding import PartitionSpec as P

F = 16384
S = 2
MESH = pl.DeviceIdType.MESH
Z = 4
NT = 8
TILE = 256

penalty = 1.0
sharpness = 1.0


def latent_grad(dact, sumsq, act, gates):
    norm = jnp.sqrt(sumsq)[None, :]
    tanh_val = jnp.tanh(sharpness * act * norm)
    return (gates * (dact + penalty * sharpness * norm * (1.0 - tanh_val * tanh_val))).astype(
        jnp.bfloat16
    )


def local_any(inputs, w_enc, b_enc, masks, w_dec, errors, target_of):
    block = w_enc.shape[1]
    source = lax.axis_index("lat") * block // F
    slot = lax.axis_index("tgt")
    slots = jnp.arange(target_of.shape[0], dtype=jnp.int32)
    layer = jnp.sum(jnp.where(slots == slot, target_of, 0))
    flag = (layer >= source).astype(jnp.float32)
    gathered = lax.all_gather(inputs, "lat", axis=0, tiled=True)
    own = lax.dynamic_index_in_dim(gathered, source, 1, keepdims=False)
    partial_pre = jnp.dot(own, w_enc, preferred_element_type=jnp.float32)
    gates = masks.astype(jnp.float32)
    weights = w_dec[0]
    squares = flag * jnp.einsum("cd,cd->c", weights, weights, preferred_element_type=jnp.float32)
    term = flag * lax.dot_general(
        lax.all_gather(errors, "lat", axis=1, tiled=True)[0],
        weights,
        (((1,), (1,)), ((), ())),
        preferred_element_type=jnp.float32,
    )
    pre = lax.psum(partial_pre, "tgt") + b_enc[None, :]
    act = gates * pre
    dact, sumsq = lax.psum((term, squares), "tgt")
    grad = latent_grad(dact, sumsq, act, gates)
    grad_bias = jnp.sum(grad.astype(jnp.float32), axis=0)
    grad_enc = lax.dot_general(
        own, grad, (((0,), (0,)), ((), ())), preferred_element_type=jnp.float32
    )
    picker = (jnp.arange(S, dtype=jnp.int32) == source).astype(jnp.float32)
    part = lax.dot_general(
        grad, w_enc, (((1,), (1,)), ((), ())), preferred_element_type=jnp.float32
    )
    grad_in = lax.psum_scatter(
        part[:, None, :] * picker[None, :, None], "lat", scatter_dimension=0, tiled=True
    )
    return (grad_enc, grad_bias, grad_in)


CHUNKS = 3


def tile_grad(dact, sumsq, act, gates):
    norm = jnp.sqrt(sumsq)
    tanh_val = jnp.tanh(sharpness * act * norm)
    return gates * (dact + penalty * sharpness * norm * (1.0 - tanh_val * tanh_val))


def kernel(
    x_hbm, we_hbm, b_hbm, mask_hbm, wd_hbm, e_hbm, target_ref,
    g_out, own_out, in_out,
    we, wd, mask, b_ref, x_raw, x_in, xs, es, xg, own_t, eg, et, pre_send, pre_got, dact_send, dact_got,
    sq_own, sq_got, pre_own, dact_own, g_own, g_got, acc_t,
    rs, rc, sums, ry, u, rz,
    load_sem, xz_s, xz_r, xy_s, xy_r, xc_s, xc_r, ez_s, ez_r, ey_s, ey_r, ec_s, ec_r,
    pre_s, pre_r, dact_s, dact_r, sq_s, sq_r, g_s, g_r, rc_s, rc_r, ry_s, ry_r, rz_s, rz_r, out_sem,
):
    f32 = jnp.float32
    half = mask.shape[1]
    me = lax.axis_index("lat")
    t = lax.axis_index("tgt")
    z, y, c = me // 4, (me // 2) % 2, me % 2
    source = z // (Z // S)
    far = [(z + k) % Z for k in range(Z)]
    near = [(z + Z - k) % Z for k in range(Z)]

    def lat_of(zz, yy, cc):
        return (zz * 2 + yy) * 2 + cc

    x_peer = (me, 1 - t)
    y_peer = (lat_of(z, 1 - y, c), t)
    c_peer = (lat_of(z, y, 1 - c), t)
    z_peer = [(lat_of(far[k], y, c), t) for k in range(Z)]

    def we_load(j):
        return pltpu.make_async_copy(
            we_hbm.at[:, pl.ds(pl.multiple_of(j * TILE, TILE), TILE)], we.at[j], load_sem.at[j]
        )

    def wd_load(j):
        return pltpu.make_async_copy(
            wd_hbm.at[0, pl.ds(pl.multiple_of(j * TILE, TILE), TILE)], wd.at[j], load_sem.at[NT + j]
        )

    def mask_load(j):
        return pltpu.make_async_copy(
            mask_hbm.at[pl.ds(t * half, half), pl.ds(pl.multiple_of(j * TILE, TILE), TILE)],
            mask.at[j],
            load_sem.at[2 * NT + j],
        )

    e_load = pltpu.make_async_copy(e_hbm.at[0], es.at[c, z * 2 + y], load_sem.at[3 * NT])
    x_load = pltpu.make_async_copy(x_hbm, x_raw, load_sem.at[3 * NT + 1])
    b_load = pltpu.make_async_copy(b_hbm, b_ref, load_sem.at[3 * NT + 2])
    x_load.start()
    e_load.start()
    for j in range(NT):
        we_load(j).start()

    barrier = pltpu.get_barrier_semaphore()
    for peer in [x_peer, y_peer, c_peer] + z_peer[1:]:
        pl.semaphore_signal(barrier, inc=1, device_id=peer, device_id_type=MESH)
    x_load.wait()
    raw = x_raw[...].astype(f32)
    for layer in range(S):
        x_in[layer] = raw[:, layer, :].astype(jnp.bfloat16)
    xs[c, z * 2 + y] = x_in[source]
    pl.semaphore_wait(barrier, Z + 2)

    def remote(src, dst, send, recv, peer):
        return pltpu.make_async_remote_copy(
            src_ref=src, dst_ref=dst, send_sem=send, recv_sem=recv, device_id=peer, device_id_type=MESH
        )

    here = z * 2 + y
    xz = [
        remote(x_in.at[far[k] // (Z // S)], xs.at[c, here], xz_s.at[k], xz_r.at[k], z_peer[k])
        for k in range(1, Z)
    ]
    ez = [remote(e_hbm.at[0], es.at[c, here], ez_s.at[k], ez_r.at[k], z_peer[k]) for k in range(1, Z)]
    for copy in xz:
        copy.start()
    for j in range(NT):
        wd_load(j).start()

    def along_y(buf, s, r):
        return [
            remote(buf.at[c, near[k] * 2 + y], buf.at[c, near[k] * 2 + y], s.at[k], r.at[k], y_peer)
            for k in range(Z)
        ]

    def along_c(buf, s, r):
        return [
            remote(
                buf.at[c, pl.ds(near[k] * 2, 2)], buf.at[c, pl.ds(near[k] * 2, 2)], s.at[k], r.at[k], c_peer
            )
            for k in range(Z)
        ]

    xy, xc = along_y(xs, xy_s, xy_r), along_c(xs, xc_s, xc_r)
    ey, ec = along_y(es, ey_s, ey_r), along_c(es, ec_s, ec_r)

    def z_to_y(along_z, y_copies):
        y_copies[0].start()
        for k in range(1, Z):
            along_z[k - 1].wait_recv()
            y_copies[k].start()

    def y_to_c(y_copies, c_copies):
        for k in range(Z):
            y_copies[k].wait_recv()
            c_copies[k].start()

    def squares(j):
        wd_load(j).wait()
        total = jnp.zeros((TILE, 128), f32)
        for at in range(0, wd.shape[2], 128):
            w = wd[j, :, at : at + 128].astype(f32)
            total = total + w * w
        sq_own[j] = flag * jnp.sum(total.T, axis=0, keepdims=True)

    flag = jnp.where(target_ref[t] >= source, 1.0, 0.0).astype(f32)

    z_to_y(xz, xy)
    for copy in ez:
        copy.start()
    squares(0)
    y_to_c(xy, xc)
    for j in range(NT):
        mask_load(j).start()
    b_load.start()
    squares(1)
    e_load.wait()
    z_to_y(ez, ey)
    pl.loop(2, 4)(squares)
    for copy in xc:
        copy.wait_recv()

    def tokens_of(buf, out):
        for q in range(Z * 2):
            at = (q + t * Z) % (Z * 2)
            pair = jnp.concatenate([buf[0, at].astype(f32), buf[1, at].astype(f32)], axis=0)
            out[q * 16 : q * 16 + 16] = pair.astype(jnp.bfloat16)

    tokens_of(xs, xg)

    def pre_copy(j):
        return remote(pre_send.at[j], pre_got.at[j], pre_s.at[j], pre_r.at[j], x_peer)

    def pre_tile(j):
        we_load(j).wait()
        part = jnp.dot(xg[...], we[j], preferred_element_type=f32)
        pre_own[j] = part[:half]
        pre_send[j] = part[half:].astype(jnp.bfloat16)
        pre_copy(j).start()

    pl.loop(0, NT)(pre_tile)
    y_to_c(ey, ec)
    pl.loop(4, NT)(squares)
    sq_copy = remote(sq_own, sq_got, sq_s.at[0], sq_r.at[0], x_peer)
    sq_copy.start()
    for at in range(0, xg.shape[1], 128):
        own_t[at : at + 128] = xg[:, at : at + 128].astype(f32).T.astype(jnp.bfloat16)
    own_store = pltpu.make_async_copy(own_t, own_out, out_sem.at[2 * NT])
    own_store.start()
    for copy in ec:
        copy.wait_recv()
    tokens_of(es, eg)
    for at in range(0, eg.shape[1], 128):
        et[at : at + 128] = eg[:, at : at + 128].astype(f32).T.astype(jnp.bfloat16)

    def dact_copy(j):
        return remote(dact_send.at[j], dact_got.at[j], dact_s.at[j], dact_r.at[j], x_peer)

    def dact_tile(j):
        part = flag * jnp.dot(wd[j], et[...], preferred_element_type=f32).T
        dact_own[j] = part[:half]
        dact_send[j] = part[half:].astype(jnp.bfloat16)
        dact_copy(j).start()

    pl.loop(0, NT)(dact_tile)
    b_load.wait()
    sq_copy.wait_recv()

    def g_copy(j):
        return remote(g_own.at[j], g_got.at[j], g_s.at[j], g_r.at[j], x_peer)

    def g_store(h, j):
        buf = g_own if h == 0 else g_got
        at = pl.ds(pl.multiple_of(j * TILE, TILE), TILE)
        return pltpu.make_async_copy(
            buf.at[j], g_out.at[h * half : h * half + half, at], out_sem.at[h * NT + j]
        )

    def input_part(w, grad):
        return jnp.dot(w, grad.T.astype(jnp.bfloat16), preferred_element_type=f32)

    acc_t[...] = jnp.zeros_like(acc_t)

    def grad_tile(j):
        mask_load(j).wait()
        pre_copy(j).wait_recv()
        dact_copy(j).wait_recv()
        gates = mask[j].astype(f32)
        bias = b_ref[:, pl.ds(pl.multiple_of(j * TILE, TILE), TILE)]
        pre = pre_own[j] + pre_got[j].astype(f32) + bias
        dact = dact_own[j] + dact_got[j].astype(f32)
        grad = tile_grad(dact, sq_own[j] + sq_got[j], gates * pre, gates).astype(jnp.bfloat16)
        g_own[j] = grad
        g_copy(j).start()
        g_store(0, j).start()
        acc_t[0] += input_part(we[j], grad.astype(f32))

    pl.loop(0, NT)(grad_tile)

    chunks = range(rs.shape[1])
    wide = rs.shape[-1]
    slots = [(h, d) for h in range(2) for d in chunks]

    def sum_copies(src, dst, s, r, other, peer):
        return {
            (h, d): remote(src.at[h, d, other], dst.at[h, d], s.at[h, d], r.at[h, d], peer)
            for h, d in slots
        }

    to_c = sum_copies(rs, rc, rc_s, rc_r, 1 - c, c_peer)
    to_y = sum_copies(sums, ry, ry_s, ry_r, 1 - y, y_peer)
    to_z = {
        (d, k): remote(u.at[d, far[k]], rz.at[d, k], rz_s.at[d, k], rz_r.at[d, k], z_peer[k])
        for d in chunks
        for k in range(1, Z)
    }

    def over_c(h, d, part):
        part = part.T
        for b in range(half // 8):
            rs[h, d, b % 2, (b // 2) % 2, b // 4] = part[b * 8 : b * 8 + 8]
        to_c[h, d].start()

    def over_y(h, d):
        to_c[h, d].wait_recv()
        sums[h, d, 1 - y] = (rs[h, d, c, 1 - y] + rc[h, d, 1 - y]).astype(jnp.bfloat16)
        to_y[h, d].start()

    def over_z(h, d):
        group = t if h == 0 else 1 - t
        to_y[h, d].wait_recv()
        total = rs[h, d, c, y] + rc[h, d, y] + ry[h, d].astype(f32)
        for zz in range(Z // 2):
            u[d, group * (Z // 2) + zz] = total[zz]
        for k in range(1, Z):
            pl.when(far[k] // (Z // 2) == group)(to_z[d, k].start)

    def got_tile(j):
        g_copy(j).wait_recv()
        g_store(1, j).start()
        acc_t[1] += input_part(we[j], g_got[j].astype(f32))

    for d in chunks:
        over_c(0, d, acc_t[0, d * wide : (d + 1) * wide])
    pl.loop(0, 2)(got_tile)
    for d in chunks:
        over_y(0, d)
    pl.loop(2, 5)(got_tile)
    for d in chunks:
        over_z(0, d)
    pl.loop(5, NT - 1)(got_tile)
    g_copy(NT - 1).wait_recv()
    g_store(1, NT - 1).start()
    last = g_got[NT - 1].astype(f32)
    for d in chunks:
        at = slice(d * wide, (d + 1) * wide)
        over_c(1, d, acc_t[1, at] + input_part(we[NT - 1, at], last))
    for d in chunks:
        over_y(1, d)
    for d in chunks:
        over_z(1, d)
    for d in chunks:
        terms = [u[d, z]]
        for k in range(1, Z):
            to_z[d, k].wait_recv()
            terms.append(rz[d, k])
        for layer in range(S):
            total = jnp.zeros_like(terms[0])
            for k in range(Z):
                total = total + jnp.where(near[k] // (Z // S) == layer, terms[k], 0.0)
            in_out[layer, :, d * wide : (d + 1) * wide] = total

    for copy in xz + ez + xy + xc + ey + ec + [sq_copy] + [*to_c.values(), *to_y.values(), *to_z.values()]:
        copy.wait_send()
    for j in range(NT):
        pre_copy(j).wait_send()
        dact_copy(j).wait_send()
        g_copy(j).wait_send()
        g_store(0, j).wait()
        g_store(1, j).wait()
    own_store.wait()


def encoder_kernel(own_ref, g_ref, in_ref, enc_hbm, bias_out, in_out, enc, sem):
    step = enc.shape[1]

    def store(i):
        return pltpu.make_async_copy(enc.at[i], enc_hbm.at[pl.ds(i * step, step)], sem.at[i])

    @pl.loop(0, enc.shape[0])
    def _(i):
        enc[i] = jnp.dot(
            own_ref[pl.ds(i * step, step)], g_ref[...], preferred_element_type=jnp.float32
        )
        store(i).start()

    half = g_ref.shape[0] // 2
    sums = [
        jnp.sum(g_ref[h * half : h * half + half].astype(jnp.float32), axis=0, keepdims=True)
        for h in range(2)
    ]
    bias_out[...] = sums[0] + sums[1]
    for layer in range(S):
        in_out[:, layer, :] = in_ref[layer]
    for i in range(enc.shape[0]):
        store(i).wait()


def local_kernel(inputs, w_enc, b_enc, masks, w_dec, errors, target_of):
    rows, _, width = inputs.shape
    tokens, block = masks.shape
    full = w_dec.shape[2]
    f32, bf16 = jnp.float32, jnp.bfloat16
    vmem = pltpu.VMEM
    dma = pltpu.SemaphoreType.DMA
    hbm = pl.BlockSpec(memory_space=pltpu.HBM)
    free, whole = pl.BlockSpec(memory_space=pl.ANY), pl.BlockSpec(memory_space=pltpu.VMEM)
    tiles = (NT, tokens // 2, TILE)
    wide = width // CHUNKS
    grad, own_t, grad_in = pl.pallas_call(
        kernel,
        out_shape=(
            jax.ShapeDtypeStruct((tokens, block), bf16),
            jax.ShapeDtypeStruct((width, tokens), bf16),
            jax.ShapeDtypeStruct((S, rows, width), f32),
        ),
        in_specs=[hbm] * 6 + [pl.BlockSpec(memory_space=pltpu.SMEM)],
        out_specs=(free, free, whole),
        scratch_shapes=[
            vmem((NT, width, TILE), bf16),
            vmem((NT, TILE, full), bf16),
            vmem(tiles, jnp.int32),
            vmem((1, block), f32),
            vmem((rows, S, width), bf16),
            vmem((S, rows, width), bf16),
            vmem((2, Z * 2, rows, width), bf16),
            vmem((2, Z * 2, rows, full), bf16),
            vmem((tokens, width), bf16),
            vmem((width, tokens), bf16),
            vmem((tokens, full), bf16),
            vmem((full, tokens), bf16),
            vmem(tiles, bf16), vmem(tiles, bf16), vmem(tiles, bf16), vmem(tiles, bf16),
            vmem((NT, 1, TILE), f32), vmem((NT, 1, TILE), f32),
            vmem(tiles, f32), vmem(tiles, f32),
            vmem(tiles, bf16), vmem(tiles, bf16),
            vmem((2, width, tokens // 2), f32),
            vmem((2, CHUNKS, 2, 2, Z // 2, rows, wide), f32),
            vmem((2, CHUNKS, 2, Z // 2, rows, wide), f32),
            vmem((2, CHUNKS, 2, Z // 2, rows, wide), bf16),
            vmem((2, CHUNKS, Z // 2, rows, wide), bf16),
            vmem((CHUNKS, Z, rows, wide), f32),
            vmem((CHUNKS, Z, rows, wide), f32),
            dma((3 * NT + 3,)),
        ]
        + [dma((Z,))] * 12
        + [dma((NT,))] * 4
        + [dma((1,))] * 2
        + [dma((NT,))] * 2
        + [dma((2, CHUNKS))] * 4
        + [dma((CHUNKS, Z))] * 2
        + [dma((2 * NT + 1,))],
        compiler_params=pltpu.CompilerParams(
            collective_id=0, has_side_effects=True, vmem_limit_bytes=62 * 1024 * 1024
        ),
    )(inputs, w_enc, b_enc[None, :], masks, w_dec, errors, target_of)
    grad_enc, bias, grad_in = pl.pallas_call(
        encoder_kernel,
        out_shape=(
            jax.ShapeDtypeStruct((width, block), f32),
            jax.ShapeDtypeStruct((1, block), f32),
            jax.ShapeDtypeStruct((rows, S, width), f32),
        ),
        in_specs=[whole] * 3,
        out_specs=(free, whole, whole),
        scratch_shapes=[vmem((6, width // 6, block), f32), dma((6,))],
        compiler_params=pltpu.CompilerParams(vmem_limit_bytes=62 * 1024 * 1024),
    )(own_t, grad, grad_in)
    return grad_enc, bias[0], grad_in


def solution(mesh):
    sizes = dict(mesh.shape)
    fits = sizes["lat"] == 4 * Z and sizes["tgt"] == 2
    return jax.shard_map(
        local_kernel if fits else local_any,
        mesh=mesh,
        in_specs=(
            P("lat", None, "tgt"),
            P("tgt", "lat"),
            P("lat"),
            P(None, "lat"),
            P("tgt", "lat", None),
            P("tgt", "lat", None),
            P(),
        ),
        out_specs=(P("tgt", "lat"), P("lat"), P("lat", None, "tgt")),
        check_vma=False,
    )
```

```python
import functools

import jax
import jax.numpy as jnp
from jax import lax
from jax.experimental import pallas as pl
from jax.experimental.pallas import tpu as pltpu
from jax.sharding import PartitionSpec as P

F = 16384
S = 2
MESH = pl.DeviceIdType.MESH
Z = 4
NT = 8
TILE = 256

penalty = 1.0
sharpness = 1.0


def latent_grad(dact, sumsq, act, gates):
    norm = jnp.sqrt(sumsq)[None, :]
    tanh_val = jnp.tanh(sharpness * act * norm)
    return (gates * (dact + penalty * sharpness * norm * (1.0 - tanh_val * tanh_val))).astype(
        jnp.bfloat16
    )


def local_any(inputs, w_enc, b_enc, masks, w_dec, errors, target_of):
    block = w_enc.shape[1]
    source = lax.axis_index("lat") * block // F
    slot = lax.axis_index("tgt")
    slots = jnp.arange(target_of.shape[0], dtype=jnp.int32)
    layer = jnp.sum(jnp.where(slots == slot, target_of, 0))
    flag = (layer >= source).astype(jnp.float32)
    gathered = lax.all_gather(inputs, "lat", axis=0, tiled=True)
    own = lax.dynamic_index_in_dim(gathered, source, 1, keepdims=False)
    partial_pre = jnp.dot(own, w_enc, preferred_element_type=jnp.float32)
    gates = masks.astype(jnp.float32)
    weights = w_dec[0]
    squares = flag * jnp.einsum("cd,cd->c", weights, weights, preferred_element_type=jnp.float32)
    term = flag * lax.dot_general(
        lax.all_gather(errors, "lat", axis=1, tiled=True)[0],
        weights,
        (((1,), (1,)), ((), ())),
        preferred_element_type=jnp.float32,
    )
    pre = lax.psum(partial_pre, "tgt") + b_enc[None, :]
    act = gates * pre
    dact, sumsq = lax.psum((term, squares), "tgt")
    grad = latent_grad(dact, sumsq, act, gates)
    grad_bias = jnp.sum(grad.astype(jnp.float32), axis=0)
    grad_enc = lax.dot_general(
        own, grad, (((0,), (0,)), ((), ())), preferred_element_type=jnp.float32
    )
    picker = (jnp.arange(S, dtype=jnp.int32) == source).astype(jnp.float32)
    part = lax.dot_general(
        grad, w_enc, (((1,), (1,)), ((), ())), preferred_element_type=jnp.float32
    )
    grad_in = lax.psum_scatter(
        part[:, None, :] * picker[None, :, None], "lat", scatter_dimension=0, tiled=True
    )
    return (grad_enc, grad_bias, grad_in)


CHUNKS = 3


def tile_grad(dact, sumsq, act, gates):
    norm = jnp.sqrt(sumsq)
    tanh_val = jnp.tanh(sharpness * act * norm)
    return gates * (dact + penalty * sharpness * norm * (1.0 - tanh_val * tanh_val))


def kernel(
    x_hbm, we_hbm, b_hbm, mask_hbm, wd_hbm, e_hbm, target_ref,
    g_out, own_out, in_out,
    we, wd, mask, b_ref, x_raw, x_in, xs, es, xg, own_t, eg, et, pre_send, pre_got, dact_send, dact_got,
    sq_own, sq_got, pre_own, dact_own, g_own, g_got, acc_t,
    rs, rc, sums, ry, u, rz,
    load_sem, xz_s, xz_r, xy_s, xy_r, xc_s, xc_r, ez_s, ez_r, ey_s, ey_r, ec_s, ec_r,
    pre_s, pre_r, dact_s, dact_r, sq_s, sq_r, g_s, g_r, rc_s, rc_r, ry_s, ry_r, rz_s, rz_r, out_sem,
):
    f32 = jnp.float32
    half = mask.shape[1]
    me = lax.axis_index("lat")
    t = lax.axis_index("tgt")
    z, y, c = me // 4, (me // 2) % 2, me % 2
    source = z // (Z // S)
    far = [(z + k) % Z for k in range(Z)]
    near = [(z + Z - k) % Z for k in range(Z)]

    def lat_of(zz, yy, cc):
        return (zz * 2 + yy) * 2 + cc

    x_peer = (me, 1 - t)
    y_peer = (lat_of(z, 1 - y, c), t)
    c_peer = (lat_of(z, y, 1 - c), t)
    z_peer = [(lat_of(far[k], y, c), t) for k in range(Z)]

    def we_load(j):
        return pltpu.make_async_copy(
            we_hbm.at[:, pl.ds(pl.multiple_of(j * TILE, TILE), TILE)], we.at[j], load_sem.at[j]
        )

    def wd_load(j):
        return pltpu.make_async_copy(
            wd_hbm.at[0, pl.ds(pl.multiple_of(j * TILE, TILE), TILE)], wd.at[j], load_sem.at[NT + j]
        )

    def mask_load(j):
        return pltpu.make_async_copy(
            mask_hbm.at[pl.ds(t * half, half), pl.ds(pl.multiple_of(j * TILE, TILE), TILE)],
            mask.at[j],
            load_sem.at[2 * NT + j],
        )

    e_load = pltpu.make_async_copy(e_hbm.at[0], es.at[c, z * 2 + y], load_sem.at[3 * NT])
    x_load = pltpu.make_async_copy(x_hbm, x_raw, load_sem.at[3 * NT + 1])
    b_load = pltpu.make_async_copy(b_hbm, b_ref, load_sem.at[3 * NT + 2])
    x_load.start()
    e_load.start()
    for j in range(NT):
        we_load(j).start()

    barrier = pltpu.get_barrier_semaphore()
    for peer in [x_peer, y_peer, c_peer] + z_peer[1:]:
        pl.semaphore_signal(barrier, inc=1, device_id=peer, device_id_type=MESH)
    x_load.wait()
    raw = x_raw[...].astype(f32)
    for layer in range(S):
        x_in[layer] = raw[:, layer, :].astype(jnp.bfloat16)
    xs[c, z * 2 + y] = x_in[source]
    pl.semaphore_wait(barrier, Z + 2)

    def remote(src, dst, send, recv, peer):
        return pltpu.make_async_remote_copy(
            src_ref=src, dst_ref=dst, send_sem=send, recv_sem=recv, device_id=peer, device_id_type=MESH
        )

    here = z * 2 + y
    xz = [
        remote(x_in.at[far[k] // (Z // S)], xs.at[c, here], xz_s.at[k], xz_r.at[k], z_peer[k])
        for k in range(1, Z)
    ]
    ez = [remote(e_hbm.at[0], es.at[c, here], ez_s.at[k], ez_r.at[k], z_peer[k]) for k in range(1, Z)]
    for copy in xz:
        copy.start()
    for j in range(NT):
        wd_load(j).start()

    def along_y(buf, s, r):
        return [
            remote(buf.at[c, near[k] * 2 + y], buf.at[c, near[k] * 2 + y], s.at[k], r.at[k], y_peer)
            for k in range(Z)
        ]

    def along_c(buf, s, r):
        return [
            remote(
                buf.at[c, pl.ds(near[k] * 2, 2)], buf.at[c, pl.ds(near[k] * 2, 2)], s.at[k], r.at[k], c_peer
            )
            for k in range(Z)
        ]

    xy, xc = along_y(xs, xy_s, xy_r), along_c(xs, xc_s, xc_r)
    ey, ec = along_y(es, ey_s, ey_r), along_c(es, ec_s, ec_r)

    def z_to_y(along_z, y_copies, k):
        if k:
            along_z[k - 1].wait_recv()
        y_copies[k].start()

    def y_to_c(y_copies, c_copies, k):
        y_copies[k].wait_recv()
        c_copies[k].start()

    def squares(j):
        wd_load(j).wait()
        total = jnp.zeros((TILE, 128), f32)
        for at in range(0, wd.shape[2], 128):
            w = wd[j, :, at : at + 128].astype(f32)
            total = total + w * w
        sq_own[j] = flag * jnp.sum(total.T, axis=0, keepdims=True)

    flag = jnp.where(target_ref[t] >= source, 1.0, 0.0).astype(f32)

    for k in range(Z):
        z_to_y(xz, xy, k)
    for copy in ez:
        copy.start()
    squares(0)
    for k in range(Z):
        y_to_c(xy, xc, k)
    for j in range(NT):
        mask_load(j).start()
    b_load.start()
    e_load.wait()
    z_to_y(ez, ey, 0)
    squares(1)
    for copy in xc:
        copy.wait_recv()

    def tokens_of(buf, out):
        for q in range(Z * 2):
            at = (q + t * Z) % (Z * 2)
            pair = jnp.concatenate([buf[0, at].astype(f32), buf[1, at].astype(f32)], axis=0)
            out[q * 16 : q * 16 + 16] = pair.astype(jnp.bfloat16)

    tokens_of(xs, xg)

    def pre_copy(j):
        return remote(pre_send.at[j], pre_got.at[j], pre_s.at[j], pre_r.at[j], x_peer)

    def pre_tile(j):
        we_load(j).wait()
        part = jnp.dot(xg[...], we[j], preferred_element_type=f32)
        pre_own[j] = part[:half]
        pre_send[j] = part[half:].astype(jnp.bfloat16)
        pre_copy(j).start()

    pl.loop(0, 2)(pre_tile)
    for k in range(1, Z):
        z_to_y(ez, ey, k)
        pre_tile(k + 1)
    pl.loop(Z + 1, NT)(pre_tile)
    for k in range(Z):
        squares(k + 2)
        y_to_c(ey, ec, k)
    for copy in ec:
        copy.wait_recv()
    tokens_of(es, eg)
    for at in range(0, eg.shape[1], 128):
        et[at : at + 128] = eg[:, at : at + 128].astype(f32).T.astype(jnp.bfloat16)

    def dact_copy(j):
        return remote(dact_send.at[j], dact_got.at[j], dact_s.at[j], dact_r.at[j], x_peer)

    def dact_tile(j):
        part = flag * jnp.dot(wd[j], et[...], preferred_element_type=f32).T
        dact_own[j] = part[:half]
        dact_send[j] = part[half:].astype(jnp.bfloat16)
        dact_copy(j).start()

    @pl.loop(0, 2)
    def _(j):
        dact_tile(j)
        squares(j + NT - 2)

    sq_copy = remote(sq_own, sq_got, sq_s.at[0], sq_r.at[0], x_peer)
    sq_copy.start()

    def g_copy(j):
        return remote(g_own.at[j], g_got.at[j], g_s.at[j], g_r.at[j], x_peer)

    def g_store(h, j):
        buf = g_own if h == 0 else g_got
        at = pl.ds(pl.multiple_of(j * TILE, TILE), TILE)
        return pltpu.make_async_copy(
            buf.at[j], g_out.at[h * half : h * half + half, at], out_sem.at[h * NT + j]
        )

    def input_part(w, grad):
        return jnp.dot(w, grad.T.astype(jnp.bfloat16), preferred_element_type=f32)

    acc_t[...] = jnp.zeros_like(acc_t)

    def grad_tile(j):
        mask_load(j).wait()
        pre_copy(j).wait_recv()
        dact_copy(j).wait_recv()
        gates = mask[j].astype(f32)
        bias = b_ref[:, pl.ds(pl.multiple_of(j * TILE, TILE), TILE)]
        pre = pre_own[j] + pre_got[j].astype(f32) + bias
        dact = dact_own[j] + dact_got[j].astype(f32)
        grad = tile_grad(dact, sq_own[j] + sq_got[j], gates * pre, gates).astype(jnp.bfloat16)
        g_own[j] = grad
        g_copy(j).start()
        g_store(0, j).start()
        acc_t[0] += input_part(we[j], grad.astype(f32))

    lag = 4
    pl.loop(2, lag)(dact_tile)
    b_load.wait()
    sq_copy.wait_recv()

    @pl.loop(lag, NT)
    def _(j):
        dact_tile(j)
        grad_tile(j - lag)

    pl.loop(NT - lag, NT)(grad_tile)

    chunks = range(rs.shape[1])
    wide = rs.shape[-1]
    slots = [(h, d) for h in range(2) for d in chunks]

    def sum_copies(src, dst, s, r, other, peer):
        return {
            (h, d): remote(src.at[h, d, other], dst.at[h, d], s.at[h, d], r.at[h, d], peer)
            for h, d in slots
        }

    to_c = sum_copies(rs, rc, rc_s, rc_r, 1 - c, c_peer)
    to_y = sum_copies(sums, ry, ry_s, ry_r, 1 - y, y_peer)
    to_z = {
        (d, k): remote(u.at[d, far[k]], rz.at[d, k], rz_s.at[d, k], rz_r.at[d, k], z_peer[k])
        for d in chunks
        for k in range(1, Z)
    }

    def over_c(h, d, part):
        part = part.T
        for b in range(half // 8):
            rs[h, d, b % 2, (b // 2) % 2, b // 4] = part[b * 8 : b * 8 + 8]
        to_c[h, d].start()

    def over_y(h, d):
        to_c[h, d].wait_recv()
        sums[h, d, 1 - y] = (rs[h, d, c, 1 - y] + rc[h, d, 1 - y]).astype(jnp.bfloat16)
        to_y[h, d].start()

    def over_z(h, d):
        group = t if h == 0 else 1 - t
        to_y[h, d].wait_recv()
        total = rs[h, d, c, y] + rc[h, d, y] + ry[h, d].astype(f32)
        for zz in range(Z // 2):
            u[d, group * (Z // 2) + zz] = total[zz]
        for k in range(1, Z):
            pl.when(far[k] // (Z // 2) == group)(to_z[d, k].start)

    def got_tile(j):
        g_copy(j).wait_recv()
        g_store(1, j).start()
        acc_t[1] += input_part(we[j], g_got[j].astype(f32))

    for d in chunks:
        over_c(0, d, acc_t[0, d * wide : (d + 1) * wide])
    pl.loop(0, 2)(got_tile)
    for d in chunks:
        over_y(0, d)
    for at in range(0, xg.shape[1], 128):
        own_t[at : at + 128] = xg[:, at : at + 128].astype(f32).T.astype(jnp.bfloat16)
    own_store = pltpu.make_async_copy(own_t, own_out, out_sem.at[2 * NT])
    own_store.start()
    pl.loop(2, 5)(got_tile)
    for d in chunks:
        over_z(0, d)
    pl.loop(5, NT - 1)(got_tile)
    g_copy(NT - 1).wait_recv()
    g_store(1, NT - 1).start()
    last = g_got[NT - 1].astype(f32)
    for d in chunks:
        at = slice(d * wide, (d + 1) * wide)
        over_c(1, d, acc_t[1, at] + input_part(we[NT - 1, at], last))
    for d in chunks:
        over_y(1, d)
    for d in chunks:
        over_z(1, d)
    for d in chunks:
        terms = [u[d, z]]
        for k in range(1, Z):
            to_z[d, k].wait_recv()
            terms.append(rz[d, k])
        for layer in range(S):
            total = jnp.zeros_like(terms[0])
            for k in range(Z):
                total = total + jnp.where(near[k] // (Z // S) == layer, terms[k], 0.0)
            in_out[layer, :, d * wide : (d + 1) * wide] = total

    for copy in xz + ez + xy + xc + ey + ec + [sq_copy] + [*to_c.values(), *to_y.values(), *to_z.values()]:
        copy.wait_send()
    for j in range(NT):
        pre_copy(j).wait_send()
        dact_copy(j).wait_send()
        g_copy(j).wait_send()
        g_store(0, j).wait()
        g_store(1, j).wait()
    own_store.wait()


def encoder_kernel(own_ref, g_ref, in_ref, enc_hbm, bias_out, in_out, enc, sem):
    step = enc.shape[1]

    def store(i):
        return pltpu.make_async_copy(enc.at[i], enc_hbm.at[pl.ds(i * step, step)], sem.at[i])

    @pl.loop(0, enc.shape[0])
    def _(i):
        enc[i] = jnp.dot(
            own_ref[pl.ds(i * step, step)], g_ref[...], preferred_element_type=jnp.float32
        )
        store(i).start()

    half = g_ref.shape[0] // 2
    sums = [
        jnp.sum(g_ref[h * half : h * half + half].astype(jnp.float32), axis=0, keepdims=True)
        for h in range(2)
    ]
    bias_out[...] = sums[0] + sums[1]
    for layer in range(S):
        in_out[:, layer, :] = in_ref[layer]
    for i in range(enc.shape[0]):
        store(i).wait()


def local_kernel(inputs, w_enc, b_enc, masks, w_dec, errors, target_of):
    rows, _, width = inputs.shape
    tokens, block = masks.shape
    full = w_dec.shape[2]
    f32, bf16 = jnp.float32, jnp.bfloat16
    vmem = pltpu.VMEM
    dma = pltpu.SemaphoreType.DMA
    hbm = pl.BlockSpec(memory_space=pltpu.HBM)
    free, whole = pl.BlockSpec(memory_space=pl.ANY), pl.BlockSpec(memory_space=pltpu.VMEM)
    tiles = (NT, tokens // 2, TILE)
    wide = width // CHUNKS
    grad, own_t, grad_in = pl.pallas_call(
        kernel,
        out_shape=(
            jax.ShapeDtypeStruct((tokens, block), bf16),
            jax.ShapeDtypeStruct((width, tokens), bf16),
            jax.ShapeDtypeStruct((S, rows, width), f32),
        ),
        in_specs=[hbm] * 6 + [pl.BlockSpec(memory_space=pltpu.SMEM)],
        out_specs=(free, free, whole),
        scratch_shapes=[
            vmem((NT, width, TILE), bf16),
            vmem((NT, TILE, full), bf16),
            vmem(tiles, jnp.int32),
            vmem((1, block), f32),
            vmem((rows, S, width), bf16),
            vmem((S, rows, width), bf16),
            vmem((2, Z * 2, rows, width), bf16),
            vmem((2, Z * 2, rows, full), bf16),
            vmem((tokens, width), bf16),
            vmem((width, tokens), bf16),
            vmem((tokens, full), bf16),
            vmem((full, tokens), bf16),
            vmem(tiles, bf16), vmem(tiles, bf16), vmem(tiles, bf16), vmem(tiles, bf16),
            vmem((NT, 1, TILE), f32), vmem((NT, 1, TILE), f32),
            vmem(tiles, f32), vmem(tiles, f32),
            vmem(tiles, bf16), vmem(tiles, bf16),
            vmem((2, width, tokens // 2), f32),
            vmem((2, CHUNKS, 2, 2, Z // 2, rows, wide), f32),
            vmem((2, CHUNKS, 2, Z // 2, rows, wide), f32),
            vmem((2, CHUNKS, 2, Z // 2, rows, wide), bf16),
            vmem((2, CHUNKS, Z // 2, rows, wide), bf16),
            vmem((CHUNKS, Z, rows, wide), f32),
            vmem((CHUNKS, Z, rows, wide), f32),
            dma((3 * NT + 3,)),
        ]
        + [dma((Z,))] * 12
        + [dma((NT,))] * 4
        + [dma((1,))] * 2
        + [dma((NT,))] * 2
        + [dma((2, CHUNKS))] * 4
        + [dma((CHUNKS, Z))] * 2
        + [dma((2 * NT + 1,))],
        compiler_params=pltpu.CompilerParams(
            collective_id=0, has_side_effects=True, vmem_limit_bytes=62 * 1024 * 1024
        ),
    )(inputs, w_enc, b_enc[None, :], masks, w_dec, errors, target_of)
    grad_enc, bias, grad_in = pl.pallas_call(
        encoder_kernel,
        out_shape=(
            jax.ShapeDtypeStruct((width, block), f32),
            jax.ShapeDtypeStruct((1, block), f32),
            jax.ShapeDtypeStruct((rows, S, width), f32),
        ),
        in_specs=[whole] * 3,
        out_specs=(free, whole, whole),
        scratch_shapes=[vmem((6, width // 6, block), f32), dma((6,))],
        compiler_params=pltpu.CompilerParams(vmem_limit_bytes=62 * 1024 * 1024),
    )(own_t, grad, grad_in)
    return grad_enc, bias[0], grad_in


def solution(mesh):
    sizes = dict(mesh.shape)
    fits = sizes["lat"] == 4 * Z and sizes["tgt"] == 2
    return jax.shard_map(
        local_kernel if fits else local_any,
        mesh=mesh,
        in_specs=(
            P("lat", None, "tgt"),
            P("tgt", "lat"),
            P("lat"),
            P(None, "lat"),
            P("tgt", "lat", None),
            P("tgt", "lat", None),
            P(),
        ),
        out_specs=(P("tgt", "lat"), P("lat"), P("lat", None, "tgt")),
        check_vma=False,
    )
```

```python
import functools

import jax
import jax.numpy as jnp
from jax import lax
from jax.experimental import pallas as pl
from jax.experimental.pallas import tpu as pltpu
from jax.sharding import PartitionSpec as P

F = 16384
S = 2
MESH = pl.DeviceIdType.MESH
Z = 4
NT = 8
TILE = 256

penalty = 1.0
sharpness = 1.0


def latent_grad(dact, sumsq, act, gates):
    norm = jnp.sqrt(sumsq)[None, :]
    tanh_val = jnp.tanh(sharpness * act * norm)
    return (gates * (dact + penalty * sharpness * norm * (1.0 - tanh_val * tanh_val))).astype(
        jnp.bfloat16
    )


def local_any(inputs, w_enc, b_enc, masks, w_dec, errors, target_of):
    block = w_enc.shape[1]
    source = lax.axis_index("lat") * block // F
    slot = lax.axis_index("tgt")
    slots = jnp.arange(target_of.shape[0], dtype=jnp.int32)
    layer = jnp.sum(jnp.where(slots == slot, target_of, 0))
    flag = (layer >= source).astype(jnp.float32)
    gathered = lax.all_gather(inputs, "lat", axis=0, tiled=True)
    own = lax.dynamic_index_in_dim(gathered, source, 1, keepdims=False)
    partial_pre = jnp.dot(own, w_enc, preferred_element_type=jnp.float32)
    gates = masks.astype(jnp.float32)
    weights = w_dec[0]
    squares = flag * jnp.einsum("cd,cd->c", weights, weights, preferred_element_type=jnp.float32)
    term = flag * lax.dot_general(
        lax.all_gather(errors, "lat", axis=1, tiled=True)[0],
        weights,
        (((1,), (1,)), ((), ())),
        preferred_element_type=jnp.float32,
    )
    pre = lax.psum(partial_pre, "tgt") + b_enc[None, :]
    act = gates * pre
    dact, sumsq = lax.psum((term, squares), "tgt")
    grad = latent_grad(dact, sumsq, act, gates)
    grad_bias = jnp.sum(grad.astype(jnp.float32), axis=0)
    grad_enc = lax.dot_general(
        own, grad, (((0,), (0,)), ((), ())), preferred_element_type=jnp.float32
    )
    picker = (jnp.arange(S, dtype=jnp.int32) == source).astype(jnp.float32)
    part = lax.dot_general(
        grad, w_enc, (((1,), (1,)), ((), ())), preferred_element_type=jnp.float32
    )
    grad_in = lax.psum_scatter(
        part[:, None, :] * picker[None, :, None], "lat", scatter_dimension=0, tiled=True
    )
    return (grad_enc, grad_bias, grad_in)


CHUNKS = 3


def tile_grad(dact, sumsq, act, gates):
    norm = jnp.sqrt(sumsq)
    tanh_val = jnp.tanh(sharpness * act * norm)
    return gates * (dact + penalty * sharpness * norm * (1.0 - tanh_val * tanh_val))


def kernel(
    x_hbm, we_hbm, b_hbm, mask_hbm, wd_hbm, e_hbm, target_ref,
    g_out, own_out, in_out,
    we, wd, mask, b_ref, x_raw, x_in, xs, es, xg, own_t, eg, et, pre_send, pre_got, dact_send, dact_got,
    sq_own, sq_got, pre_own, dact_own, g_own, g_got, acc_t,
    rs, rc, sums, ry, u, rz,
    load_sem, xz_s, xz_r, xy_s, xy_r, xc_s, xc_r, ez_s, ez_r, ey_s, ey_r, ec_s, ec_r,
    pre_s, pre_r, dact_s, dact_r, sq_s, sq_r, g_s, g_r, rc_s, rc_r, ry_s, ry_r, rz_s, rz_r, out_sem,
):
    f32 = jnp.float32
    half = mask.shape[1]
    me = lax.axis_index("lat")
    t = lax.axis_index("tgt")
    z, y, c = me // 4, (me // 2) % 2, me % 2
    source = z // (Z // S)
    far = [(z + k) % Z for k in range(Z)]
    near = [(z + Z - k) % Z for k in range(Z)]

    def lat_of(zz, yy, cc):
        return (zz * 2 + yy) * 2 + cc

    x_peer = (me, 1 - t)
    y_peer = (lat_of(z, 1 - y, c), t)
    c_peer = (lat_of(z, y, 1 - c), t)
    z_peer = [(lat_of(far[k], y, c), t) for k in range(Z)]

    def we_load(j):
        return pltpu.make_async_copy(
            we_hbm.at[:, pl.ds(pl.multiple_of(j * TILE, TILE), TILE)], we.at[j], load_sem.at[j]
        )

    def wd_load(j):
        return pltpu.make_async_copy(
            wd_hbm.at[0, pl.ds(pl.multiple_of(j * TILE, TILE), TILE)], wd.at[j], load_sem.at[NT + j]
        )

    def mask_load(j):
        return pltpu.make_async_copy(
            mask_hbm.at[pl.ds(t * half, half), pl.ds(pl.multiple_of(j * TILE, TILE), TILE)],
            mask.at[j],
            load_sem.at[2 * NT + j],
        )

    e_load = pltpu.make_async_copy(e_hbm.at[0], es.at[c, z * 2 + y], load_sem.at[3 * NT])
    x_load = pltpu.make_async_copy(x_hbm, x_raw, load_sem.at[3 * NT + 1])
    b_load = pltpu.make_async_copy(b_hbm, b_ref, load_sem.at[3 * NT + 2])
    x_load.start()
    e_load.start()
    for j in range(NT):
        we_load(j).start()

    barrier = pltpu.get_barrier_semaphore()
    for peer in [x_peer, y_peer, c_peer] + z_peer[1:]:
        pl.semaphore_signal(barrier, inc=1, device_id=peer, device_id_type=MESH)
    x_load.wait()
    raw = x_raw[...].astype(f32)
    for layer in range(S):
        x_in[layer] = raw[:, layer, :].astype(jnp.bfloat16)
    xs[c, z * 2 + y] = x_in[source]
    pl.semaphore_wait(barrier, Z + 2)

    def remote(src, dst, send, recv, peer):
        return pltpu.make_async_remote_copy(
            src_ref=src, dst_ref=dst, send_sem=send, recv_sem=recv, device_id=peer, device_id_type=MESH
        )

    here = z * 2 + y
    xz = [
        remote(x_in.at[far[k] // (Z // S)], xs.at[c, here], xz_s.at[k], xz_r.at[k], z_peer[k])
        for k in range(1, Z)
    ]
    ez = [remote(e_hbm.at[0], es.at[c, here], ez_s.at[k], ez_r.at[k], z_peer[k]) for k in range(1, Z)]
    for copy in xz:
        copy.start()
    for j in range(NT):
        wd_load(j).start()

    def along_y(buf, s, r):
        return [
            remote(buf.at[c, near[k] * 2 + y], buf.at[c, near[k] * 2 + y], s.at[k], r.at[k], y_peer)
            for k in range(Z)
        ]

    def along_c(buf, s, r):
        return [
            remote(
                buf.at[c, pl.ds(near[k] * 2, 2)], buf.at[c, pl.ds(near[k] * 2, 2)], s.at[k], r.at[k], c_peer
            )
            for k in range(Z)
        ]

    xy, xc = along_y(xs, xy_s, xy_r), along_c(xs, xc_s, xc_r)
    ey, ec = along_y(es, ey_s, ey_r), along_c(es, ec_s, ec_r)

    def z_to_y(along_z, y_copies, k):
        if k:
            along_z[k - 1].wait_recv()
        y_copies[k].start()

    def y_to_c(y_copies, c_copies, k):
        y_copies[k].wait_recv()
        c_copies[k].start()

    def squares(j):
        wd_load(j).wait()
        total = jnp.zeros((TILE, 128), f32)
        for at in range(0, wd.shape[2], 128):
            w = wd[j, :, at : at + 128].astype(f32)
            total = total + w * w
        sq_own[j] = flag * jnp.sum(total.T, axis=0, keepdims=True)

    flag = jnp.where(target_ref[t] >= source, 1.0, 0.0).astype(f32)

    z_to_y(xz, xy, 0)
    for copy in ez:
        copy.start()
    e_load.wait()
    z_to_y(ez, ey, 0)
    for k in range(1, Z):
        z_to_y(xz, xy, k)
    squares(0)
    for k in range(Z):
        y_to_c(xy, xc, k)
    for j in range(NT):
        mask_load(j).start()
    b_load.start()
    for k in range(1, Z):
        z_to_y(ez, ey, k)
    for copy in xc:
        copy.wait_recv()

    def tokens_of(buf, out):
        for q in range(Z * 2):
            at = (q + t * Z) % (Z * 2)
            pair = jnp.concatenate([buf[0, at].astype(f32), buf[1, at].astype(f32)], axis=0)
            out[q * 16 : q * 16 + 16] = pair.astype(jnp.bfloat16)

    tokens_of(xs, xg)

    def pre_copy(j):
        return remote(pre_send.at[j], pre_got.at[j], pre_s.at[j], pre_r.at[j], x_peer)

    def pre_tile(j):
        we_load(j).wait()
        part = jnp.dot(xg[...], we[j], preferred_element_type=f32)
        pre_own[j] = part[:half]
        pre_send[j] = part[half:].astype(jnp.bfloat16)
        pre_copy(j).start()

    pl.loop(0, 4)(pre_tile)
    for k in range(2):
        y_to_c(ey, ec, k)
    pl.loop(4, NT)(pre_tile)
    for k in range(2, Z):
        y_to_c(ey, ec, k)
    pl.loop(1, 4)(squares)
    for copy in ec:
        copy.wait_recv()
    tokens_of(es, eg)
    for at in range(0, eg.shape[1], 128):
        et[at : at + 128] = eg[:, at : at + 128].astype(f32).T.astype(jnp.bfloat16)

    def dact_copy(j):
        return remote(dact_send.at[j], dact_got.at[j], dact_s.at[j], dact_r.at[j], x_peer)

    def dact_tile(j):
        part = flag * jnp.dot(wd[j], et[...], preferred_element_type=f32).T
        dact_own[j] = part[:half]
        dact_send[j] = part[half:].astype(jnp.bfloat16)
        dact_copy(j).start()

    @pl.loop(0, 4)
    def _(j):
        dact_tile(j)
        squares(j + 4)

    sq_copy = remote(sq_own, sq_got, sq_s.at[0], sq_r.at[0], x_peer)
    sq_copy.start()

    def g_copy(j):
        return remote(g_own.at[j], g_got.at[j], g_s.at[j], g_r.at[j], x_peer)

    def g_store(h, j):
        buf = g_own if h == 0 else g_got
        at = pl.ds(pl.multiple_of(j * TILE, TILE), TILE)
        return pltpu.make_async_copy(
            buf.at[j], g_out.at[h * half : h * half + half, at], out_sem.at[h * NT + j]
        )

    def input_part(w, grad):
        return jnp.dot(w, grad.T.astype(jnp.bfloat16), preferred_element_type=f32)

    acc_t[...] = jnp.zeros_like(acc_t)

    def grad_tile(j):
        mask_load(j).wait()
        pre_copy(j).wait_recv()
        dact_copy(j).wait_recv()
        gates = mask[j].astype(f32)
        bias = b_ref[:, pl.ds(pl.multiple_of(j * TILE, TILE), TILE)]
        pre = pre_own[j] + pre_got[j].astype(f32) + bias
        dact = dact_own[j] + dact_got[j].astype(f32)
        grad = tile_grad(dact, sq_own[j] + sq_got[j], gates * pre, gates).astype(jnp.bfloat16)
        g_own[j] = grad
        g_copy(j).start()
        g_store(0, j).start()
        acc_t[0] += input_part(we[j], grad.astype(f32))

    lag = 4
    b_load.wait()
    sq_copy.wait_recv()

    @pl.loop(lag, NT)
    def _(j):
        dact_tile(j)
        grad_tile(j - lag)

    pl.loop(NT - lag, NT)(grad_tile)

    chunks = range(rs.shape[1])
    wide = rs.shape[-1]
    slots = [(h, d) for h in range(2) for d in chunks]

    def sum_copies(src, dst, s, r, other, peer):
        return {
            (h, d): remote(src.at[h, d, other], dst.at[h, d], s.at[h, d], r.at[h, d], peer)
            for h, d in slots
        }

    to_c = sum_copies(rs, rc, rc_s, rc_r, 1 - c, c_peer)
    to_y = sum_copies(sums, ry, ry_s, ry_r, 1 - y, y_peer)
    to_z = {
        (d, k): remote(u.at[d, far[k]], rz.at[d, k], rz_s.at[d, k], rz_r.at[d, k], z_peer[k])
        for d in chunks
        for k in range(1, Z)
    }

    def over_c(h, d, part):
        part = part.T
        for b in range(half // 8):
            rs[h, d, b % 2, (b // 2) % 2, b // 4] = part[b * 8 : b * 8 + 8]
        to_c[h, d].start()

    def over_y(h, d):
        to_c[h, d].wait_recv()
        sums[h, d, 1 - y] = (rs[h, d, c, 1 - y] + rc[h, d, 1 - y]).astype(jnp.bfloat16)
        to_y[h, d].start()

    def over_z(h, d):
        group = t if h == 0 else 1 - t
        to_y[h, d].wait_recv()
        total = rs[h, d, c, y] + rc[h, d, y] + ry[h, d].astype(f32)
        for zz in range(Z // 2):
            u[d, group * (Z // 2) + zz] = total[zz]
        for k in range(1, Z):
            pl.when(far[k] // (Z // 2) == group)(to_z[d, k].start)

    def got_tile(j):
        g_copy(j).wait_recv()
        g_store(1, j).start()
        acc_t[1] += input_part(we[j], g_got[j].astype(f32))

    for d in chunks:
        over_c(0, d, acc_t[0, d * wide : (d + 1) * wide])
    pl.loop(0, 2)(got_tile)
    for d in chunks:
        over_y(0, d)
    for at in range(0, xg.shape[1], 128):
        own_t[at : at + 128] = xg[:, at : at + 128].astype(f32).T.astype(jnp.bfloat16)
    own_store = pltpu.make_async_copy(own_t, own_out, out_sem.at[2 * NT])
    own_store.start()
    pl.loop(2, 5)(got_tile)
    for d in chunks:
        over_z(0, d)
    pl.loop(5, NT - 1)(got_tile)
    g_copy(NT - 1).wait_recv()
    g_store(1, NT - 1).start()
    last = g_got[NT - 1].astype(f32)
    for d in chunks:
        at = slice(d * wide, (d + 1) * wide)
        over_c(1, d, acc_t[1, at] + input_part(we[NT - 1, at], last))
    for d in chunks:
        over_y(1, d)
    for d in chunks:
        over_z(1, d)
    for d in chunks:
        terms = [u[d, z]]
        for k in range(1, Z):
            to_z[d, k].wait_recv()
            terms.append(rz[d, k])
        for layer in range(S):
            total = jnp.zeros_like(terms[0])
            for k in range(Z):
                total = total + jnp.where(near[k] // (Z // S) == layer, terms[k], 0.0)
            in_out[layer, :, d * wide : (d + 1) * wide] = total

    for copy in xz + ez + xy + xc + ey + ec + [sq_copy] + [*to_c.values(), *to_y.values(), *to_z.values()]:
        copy.wait_send()
    for j in range(NT):
        pre_copy(j).wait_send()
        dact_copy(j).wait_send()
        g_copy(j).wait_send()
        g_store(0, j).wait()
        g_store(1, j).wait()
    own_store.wait()


def encoder_kernel(own_ref, g_ref, in_ref, enc_hbm, bias_out, in_out, enc, sem):
    step = enc.shape[1]

    def store(i):
        return pltpu.make_async_copy(enc.at[i], enc_hbm.at[pl.ds(i * step, step)], sem.at[i])

    @pl.loop(0, enc.shape[0])
    def _(i):
        enc[i] = jnp.dot(
            own_ref[pl.ds(i * step, step)], g_ref[...], preferred_element_type=jnp.float32
        )
        store(i).start()

    half = g_ref.shape[0] // 2
    sums = [
        jnp.sum(g_ref[h * half : h * half + half].astype(jnp.float32), axis=0, keepdims=True)
        for h in range(2)
    ]
    bias_out[...] = sums[0] + sums[1]
    for layer in range(S):
        in_out[:, layer, :] = in_ref[layer]
    for i in range(enc.shape[0]):
        store(i).wait()


def local_kernel(inputs, w_enc, b_enc, masks, w_dec, errors, target_of):
    rows, _, width = inputs.shape
    tokens, block = masks.shape
    full = w_dec.shape[2]
    f32, bf16 = jnp.float32, jnp.bfloat16
    vmem = pltpu.VMEM
    dma = pltpu.SemaphoreType.DMA
    hbm = pl.BlockSpec(memory_space=pltpu.HBM)
    free, whole = pl.BlockSpec(memory_space=pl.ANY), pl.BlockSpec(memory_space=pltpu.VMEM)
    tiles = (NT, tokens // 2, TILE)
    wide = width // CHUNKS
    grad, own_t, grad_in = pl.pallas_call(
        kernel,
        out_shape=(
            jax.ShapeDtypeStruct((tokens, block), bf16),
            jax.ShapeDtypeStruct((width, tokens), bf16),
            jax.ShapeDtypeStruct((S, rows, width), f32),
        ),
        in_specs=[hbm] * 6 + [pl.BlockSpec(memory_space=pltpu.SMEM)],
        out_specs=(free, free, whole),
        scratch_shapes=[
            vmem((NT, width, TILE), bf16),
            vmem((NT, TILE, full), bf16),
            vmem(tiles, jnp.int32),
            vmem((1, block), f32),
            vmem((rows, S, width), bf16),
            vmem((S, rows, width), bf16),
            vmem((2, Z * 2, rows, width), bf16),
            vmem((2, Z * 2, rows, full), bf16),
            vmem((tokens, width), bf16),
            vmem((width, tokens), bf16),
            vmem((tokens, full), bf16),
            vmem((full, tokens), bf16),
            vmem(tiles, bf16), vmem(tiles, bf16), vmem(tiles, bf16), vmem(tiles, bf16),
            vmem((NT, 1, TILE), f32), vmem((NT, 1, TILE), f32),
            vmem(tiles, f32), vmem(tiles, f32),
            vmem(tiles, bf16), vmem(tiles, bf16),
            vmem((2, width, tokens // 2), f32),
            vmem((2, CHUNKS, 2, 2, Z // 2, rows, wide), f32),
            vmem((2, CHUNKS, 2, Z // 2, rows, wide), f32),
            vmem((2, CHUNKS, 2, Z // 2, rows, wide), bf16),
            vmem((2, CHUNKS, Z // 2, rows, wide), bf16),
            vmem((CHUNKS, Z, rows, wide), f32),
            vmem((CHUNKS, Z, rows, wide), f32),
            dma((3 * NT + 3,)),
        ]
        + [dma((Z,))] * 12
        + [dma((NT,))] * 4
        + [dma((1,))] * 2
        + [dma((NT,))] * 2
        + [dma((2, CHUNKS))] * 4
        + [dma((CHUNKS, Z))] * 2
        + [dma((2 * NT + 1,))],
        compiler_params=pltpu.CompilerParams(
            collective_id=0, has_side_effects=True, vmem_limit_bytes=62 * 1024 * 1024
        ),
    )(inputs, w_enc, b_enc[None, :], masks, w_dec, errors, target_of)
    grad_enc, bias, grad_in = pl.pallas_call(
        encoder_kernel,
        out_shape=(
            jax.ShapeDtypeStruct((width, block), f32),
            jax.ShapeDtypeStruct((1, block), f32),
            jax.ShapeDtypeStruct((rows, S, width), f32),
        ),
        in_specs=[whole] * 3,
        out_specs=(free, whole, whole),
        scratch_shapes=[vmem((6, width // 6, block), f32), dma((6,))],
        compiler_params=pltpu.CompilerParams(vmem_limit_bytes=62 * 1024 * 1024),
    )(own_t, grad, grad_in)
    return grad_enc, bias[0], grad_in


def solution(mesh):
    sizes = dict(mesh.shape)
    fits = sizes["lat"] == 4 * Z and sizes["tgt"] == 2
    return jax.shard_map(
        local_kernel if fits else local_any,
        mesh=mesh,
        in_specs=(
            P("lat", None, "tgt"),
            P("tgt", "lat"),
            P("lat"),
            P(None, "lat"),
            P("tgt", "lat", None),
            P("tgt", "lat", None),
            P(),
        ),
        out_specs=(P("tgt", "lat"), P("lat"), P("lat", None, "tgt")),
        check_vma=False,
    )
```
